32 devices in a mesh: dp: 8 (over z, core), loop: 4 (over y, x).
Axes of the slice: x: 2, y: 2, z: 4, core: 2. Of those that a mesh axis runs over, the one named last changes fastest.
Arguments:
- crop_tokens: bfloat16 [2048, 64, 1152], P(('dp', 'loop')), may hold values from -6 to 6
- crop_lengths: int32 [32, 64], P(('dp', 'loop')), may hold values from 1 to 64, 3072 in all within a row
- crop_owner: int32 [2048, 1], P(('dp', 'loop')), may hold values from 0 to 7; in each aligned block of 64 rows (0 to 63, 64 to 127, ...) at most 16 rows name the same one
- crop_slot: int32 [2048], P(('dp', 'loop')), may hold values from 0 to 31
- base_tokens: bfloat16 [1024, 32, 1152], P(('dp', 'loop')), may hold values from -1024 to 1024
- key_probe: bfloat16 [1152, 16], replicated, may hold values from -1 to 1
- value_weight: bfloat16 [1152, 1152], replicated, may hold values from -0.1875 to 0.1875
- out_weight: bfloat16 [1152, 1152], replicated, may hold values from -0.1875 to 0.1875
- text_embed: bfloat16 [1024, 1152], P(('dp', 'loop')), may hold values from -6 to 6
- pair_labels: int32 [1024], P(('dp', 'loop')), may hold values from 0 to 31
- logit_scale: float32 [1], replicated, may hold values from 2 to 8
- logit_bias: float32 [1], replicated, may hold values from -4 to -1
Outputs:
- image_embed: bfloat16 [1024, 1152], P(('dp', 'loop'))
- image_grad: float32 [1024, 1152], P(('dp', 'loop'))
- text_grad: float32 [1024, 1152], P(('dp', 'loop'))
The draws below stay inside these ranges and needn't reach their ends.
Inputs may be any that keep to these rules, and one draw needn't show every extreme that they name: `crop_owner`: at most 16 of the crops of one device name the same owner, and in every draw the crops of some device name one owner exactly 16 times. `crop_lengths`: the lengths of one device's crops sum to 3072 and the longest is exactly 64.
All inputs are finite; a program needn't handle non-finite values.
Results may differ from the reference program's by a relative error of at most 0.01.
Values may be sent and summed in bfloat16 or wider, within the bound.
A program may use at most 192 MiB of HBM per device.

```python
import math
import jax
import jax.numpy as jnp
import numpy as np
from jax import lax

D = 1152
HEADS = 16
HEAD_DIM = 72
IMG_DEV = 32
CROP_TOK = 64
BASE_TOK = 32
CROPS_DEV = 64
CAP = 16
PAIRS = 1024
CROPS = 2048
GROUP = 128
N_DP = 8
N_LOOP = 4


def probe_draw(key):
    probe_key = jax.random.fold_in(key, 17)
    spread = math.sqrt(HEAD_DIM / D)
    limit = min(4.0, 1.0 / spread)
    return jax.random.truncated_normal(probe_key, -limit, limit, (D, HEADS), jnp.float32) * spread


def draw_key_probe(key, part):
    return probe_draw(key).astype(jnp.bfloat16)


def draw_base_tokens(key, part):
    noise_key = jax.random.fold_in(key, 23)
    return jax.random.truncated_normal(noise_key, -6.0, 6.0, (PAIRS, BASE_TOK, D), jnp.float32).astype(jnp.bfloat16)


def with_ends(drawn, stream_key, low, top_value):
    longest = drawn.shape.index(max(drawn.shape))
    spots = []
    for shift in (0, 1):
        where = [jax.random.randint(jax.random.fold_in(stream_key, axis), (), 0, length) for axis, length in enumerate(drawn.shape)]
        where[longest] = (where[longest] + shift) % drawn.shape[longest]
        spots.append(tuple(where))
    return drawn.at[spots[0]].set(low).at[spots[1]].set(top_value)


def level_of(stream_key, extent, split, low, largest):
    def one(dim, shards_of):
        steps = jax.random.uniform(jax.random.fold_in(jax.random.fold_in(stream_key, 6), dim), (shards_of,), jnp.float32, low / len(split), largest / len(split))
        return jnp.repeat(jnp.exp(steps), extent[dim] // shards_of).reshape((-1,) + (1,) * (len(extent) - dim - 1))

    loudness = one(*split[0])
    for cut in split[1:]:
        loudness = loudness * one(*cut)
    return loudness


def rank_table(amount, lean):
    portions = [(1 << 20) // math.isqrt(grade ** lean) + 1 for grade in range(1, amount + 1)]
    scale = 1 + sum(portions) // (1 << 30)
    return np.cumsum(np.array([max(1, weight // scale) for weight in portions]))


def ranked_ids(stream_key, extent, amount, lean):
    grid = rank_table(amount, lean)
    lot = jax.random.randint(jax.random.fold_in(stream_key, 1), extent, 0, int(grid[amount - 1]))
    standing = jnp.searchsorted(jnp.asarray(grid, jnp.int32), lot, side="right")
    return jax.random.permutation(jax.random.fold_in(stream_key, 2), amount)[standing].astype(jnp.int32)


def length_profile(count, total, bound, lean):
    portions = [(1 << 20) // math.isqrt(standing ** lean) + 1 for standing in range(2, count + 1)]
    surplus, counts = total - bound - (count - 1), [1] * (count - 1)
    while surplus > 0:
        free = [i for i in range(count - 1) if counts[i] < bound]
        mass, budget = sum([portions[i] for i in free]), surplus
        for i in free:
            addition = min(bound - counts[i], max(1, budget * portions[i] // mass), surplus)
            counts[i] = counts[i] + addition
            surplus = surplus - addition
    return np.array([bound] + counts)


def ragged(stream_key, count, total, most, slope):
    if count == 2:
        one = jax.random.randint(stream_key, (), max(1, total - most), min(most, total - 1) + 1)
        return jnp.stack([one, total - one])
    sizes = jnp.asarray(length_profile(count, total, most, slope), jnp.int32)
    pairs = (count - 1) // 2
    donor, sink = sizes[1:1 + 2 * pairs:2], sizes[2:2 + 2 * pairs:2]
    margin = jnp.minimum(donor - 1, most - sink)
    moved = jax.random.randint(jax.random.fold_in(stream_key, 1), (pairs,), 0, 1 << 20) % (margin + 1)
    sizes = sizes.at[1:1 + 2 * pairs:2].set(donor - moved).at[2:2 + 2 * pairs:2].set(sink + moved)
    return sizes[jax.random.permutation(jax.random.fold_in(stream_key, 2), count)]


def shared_out(key, own, number, rows, number_of, top, most, slope):
    order = jax.random.permutation(key, number_of)
    heavy_load, ordinary = portions_of(number_of, rows * top, most, slope, True), portions_of(number_of, rows * top, most, slope, False)
    places = jnp.arange(number_of)

    def named(sizes, rotation):
        used = int((sizes > 0).sum())
        fixed = max(1, used // 4)
        moved = fixed + (places - fixed + rotation * (used - fixed)) % max(1, number_of - fixed)
        return jnp.zeros((number_of,), jnp.int32).at[order[jnp.where(places < fixed, places, moved)]].set(jnp.asarray(sizes, jnp.int32))

    sizes = jnp.where(number % 4 == 0, named(heavy_load, number // 4), named(ordinary, number - number // 4 - 1))
    mixed = jax.random.permutation(jax.random.fold_in(own, 3), number_of)
    giver, receiver = mixed[0:number_of // 2 * 2:2], mixed[1:number_of // 2 * 2:2]
    room = jnp.minimum(sizes[giver] - 1, most - sizes[receiver]) // 2
    room = jnp.where((giver == order[0]) | (receiver == order[0]) | (sizes[receiver] == 0), 0, jnp.maximum(room, 0))
    moved = jax.random.randint(jax.random.fold_in(own, 4), (number_of // 2,), 0, 1 << 20) % (room + 1)
    sizes = sizes.at[giver].add(-moved).at[receiver].add(moved)
    items = jnp.searchsorted(jnp.cumsum(sizes), jnp.arange(rows * top), side="right").astype(jnp.int32)
    table = items.reshape(top, rows).T
    table = table[jax.random.permutation(jax.random.fold_in(own, 1), rows)]
    rotation = jax.random.randint(jax.random.fold_in(own, 2), (rows, 1), 0, top)
    return jnp.take_along_axis(table, (jnp.arange(top)[None, :] + rotation) % top, axis=1)


def portions_of(amount, total, most, skew, full):
    portions = [(1 << 20) // math.isqrt(rank ** skew) + 1 for rank in range(1, amount + 1)]
    largest = most if full else min(most, max(-(-total // amount), total * portions[0] // sum(portions)))
    least = 1 if total - largest >= amount - 1 else 0
    holding, surplus = [largest] + [least] * (amount - 1), total - largest - least * (amount - 1)
    while surplus > 0:
        free = [i for i in range(1, amount) if holding[i] < largest] or [i for i in range(1, amount) if holding[i] < most]
        mass, remaining = sum([portions[i] for i in free]), surplus
        for i in free:
            addition = min(most - holding[i], max(1, remaining * portions[i] // mass), surplus)
            holding[i] = holding[i] + addition
            surplus = surplus - addition
    return np.array(holding)


def noise(own_key, shape, scale, most, split=(), kind=jnp.bfloat16):
    gain = level_of(own_key, shape, split, -0.22, 0.18) if split else 1.0
    values = jax.random.normal(own_key, shape, jnp.float32) * scale * gain
    return jnp.minimum(jnp.maximum(values, -most), most).astype(kind)


def setup_inputs(seed: int = 0) -> dict:
    seeds = jax.random.split(jax.random.key(seed), 13)
    crop_tokens = noise(seeds[0], (CROPS, CROP_TOK, D), 1.0, 6.0, ((0, 32),))
    crop_lengths = jax.vmap(lambda own: ragged(own, CROPS_DEV, 3 * CROPS_DEV * CROP_TOK // 4, CROP_TOK, 2))(jax.random.split(seeds[1], (N_DP * N_LOOP))).reshape((N_DP * N_LOOP, CROPS_DEV)).astype(jnp.int32)
    crop_owner_keys = jax.random.split(jax.random.fold_in(seeds[2], 1), CROPS // CROPS_DEV)
    crop_owner_turns = jax.random.permutation(jax.random.fold_in(seeds[2], 3), CROPS // CROPS_DEV)
    crop_owner = jax.vmap(lambda own, number: shared_out(jax.random.fold_in(seeds[2], 2), own, number, CROPS_DEV, N_DP, 1, CAP, 2))(crop_owner_keys, crop_owner_turns).reshape((CROPS, 1))
    crop_slot = with_ends(jax.random.randint(seeds[3], (CROPS,), 0, IMG_DEV), jax.random.fold_in(seeds[3], 1), 0, IMG_DEV - 1).astype(jnp.int32)
    base_tokens = draw_base_tokens(jax.random.fold_in(seeds[12], 71), 0)
    key_probe = draw_key_probe(jax.random.fold_in(seeds[12], 71), 0)
    value_weight = noise(seeds[6], (D, D), D ** -0.5, 0.1875)
    out_weight = noise(seeds[7], (D, D), D ** -0.5, 0.1875)
    text_embed = noise(seeds[8], (PAIRS, D), 1.0, 6.0, ((0, 32),))
    pair_labels = with_ends(ranked_ids(seeds[9], (PAIRS,), GROUP // 4, 2), jax.random.fold_in(seeds[9], 3), 0, (GROUP // 4) - 1).astype(jnp.int32)
    logit_scale = jnp.clip(jnp.exp(jax.random.uniform(seeds[10], (1,), jnp.float32, math.log(2.0), math.log(8.0))), 2.0, 8.0)
    logit_bias = jnp.clip(jax.random.uniform(seeds[11], (1,), jnp.float32, -4.0, -1.0), -4.0, -1.0)
    return dict(crop_tokens=crop_tokens, crop_lengths=crop_lengths, crop_owner=crop_owner, crop_slot=crop_slot, base_tokens=base_tokens, key_probe=key_probe, value_weight=value_weight, out_weight=out_weight, text_embed=text_embed, pair_labels=pair_labels, logit_scale=logit_scale, logit_bias=logit_bias)


highest = lax.Precision.HIGHEST
norm_eps = 1e-06

def unit_rows(matrix):
    return matrix * lax.rsqrt(lax.optimization_barrier(jnp.sum(matrix * matrix, axis=1, keepdims=True)) + norm_eps)

def reference(crop_tokens, crop_lengths, crop_owner, crop_slot, base_tokens, key_probe, value_weight, out_weight, text_embed, pair_labels, logit_scale, logit_bias):
    crop_count = crop_tokens.shape[0]
    pair_count = base_tokens.shape[0]
    crop_index = jnp.arange(crop_count, dtype=jnp.int32)
    loop_pos = (crop_index // CROPS_DEV % N_LOOP).astype(jnp.int32)
    pair_of = ((crop_owner[:, 0] * N_LOOP + loop_pos) * IMG_DEV + crop_slot).astype(jnp.int32)
    lengths = crop_lengths.reshape(-1)
    crop_scores = jnp.dot(crop_tokens.reshape(-1, D), key_probe, preferred_element_type=jnp.float32)
    crop_scores = crop_scores.reshape(crop_count, CROP_TOK, HEADS) / math.sqrt(HEAD_DIM)
    position = jnp.arange(CROP_TOK, dtype=jnp.int32)
    is_valid = (position[None, :] < lengths[:, None])[:, :, None]
    crop_max = lax.optimization_barrier(jnp.max(jnp.where(is_valid, crop_scores, -jnp.inf), axis=1))
    base_scores = jnp.dot(base_tokens.reshape(-1, D), key_probe, preferred_element_type=jnp.float32)
    base_scores = base_scores.reshape(pair_count, BASE_TOK, HEADS) / math.sqrt(HEAD_DIM)
    joint_max = lax.optimization_barrier(jnp.max(base_scores, axis=1)).at[pair_of].max(crop_max)
    crop_weight = jnp.where(is_valid, jnp.exp(crop_scores - joint_max[pair_of][:, None, :]), 0.0)
    base_weight = jnp.exp(base_scores - joint_max[:, None, :])
    denominator = lax.optimization_barrier(jnp.sum(base_weight, axis=1)) + jax.ops.segment_sum(lax.optimization_barrier(jnp.sum(crop_weight, axis=1)), pair_of, num_segments=pair_count)
    value_heads = value_weight.astype(jnp.float32).reshape(D, HEADS, HEAD_DIM)

    def weighted_values(block_pair):
        tokens, weight = block_pair
        mixed_sum = jnp.einsum('ckh,ckd->chd', weight, tokens.astype(jnp.float32), precision=highest)
        projected = jnp.einsum('chd,dhe->che', mixed_sum, value_heads, precision=highest)
        return projected.reshape(tokens.shape[0], D)
    crop_parts = lax.map(weighted_values, (crop_tokens.reshape(-1, CROPS_DEV, CROP_TOK, D), crop_weight.reshape(-1, CROPS_DEV, CROP_TOK, HEADS))).reshape(crop_count, D)
    base_parts = lax.map(weighted_values, (base_tokens.reshape(-1, IMG_DEV, BASE_TOK, D), base_weight.reshape(-1, IMG_DEV, BASE_TOK, HEADS))).reshape(pair_count, D)
    summed = base_parts + jax.ops.segment_sum(crop_parts, pair_of, num_segments=pair_count)
    pooled = (summed.reshape(pair_count, HEADS, HEAD_DIM) / denominator[:, :, None]).reshape(pair_count, D).astype(jnp.bfloat16)
    features = jnp.dot(pooled, out_weight, preferred_element_type=jnp.float32)
    image_embed = features.astype(jnp.bfloat16)
    image_unit = unit_rows(features).astype(jnp.bfloat16)
    text_unit = unit_rows(text_embed.astype(jnp.float32)).astype(jnp.bfloat16)
    image_groups = image_unit.astype(jnp.float32).reshape(N_DP, GROUP, D)
    text_groups = text_unit.astype(jnp.float32).reshape(N_DP, GROUP, D)
    label_groups = pair_labels.reshape(N_DP, GROUP)
    scale_value = logit_scale[0]
    bias_value = logit_bias[0]
    logits = scale_value * jnp.einsum('gid,gjd->gij', image_groups, text_groups, precision=highest) + bias_value
    target_sign = jnp.where(label_groups[:, :, None] == label_groups[:, None, :], 1.0, -1.0)
    grad_tile = (scale_value * (-target_sign * jax.nn.sigmoid(-target_sign * logits))).astype(jnp.bfloat16)
    grad_tile = lax.optimization_barrier(grad_tile).astype(jnp.float32)
    image_grad = jnp.einsum('gij,gjd->gid', grad_tile, text_groups, precision=highest).reshape(pair_count, D)
    text_grad = jnp.einsum('gij,gid->gjd', grad_tile, image_groups, precision=highest).reshape(pair_count, D)
    return (image_embed, image_grad, text_grad)
```

```python
import functools
import math

import jax
import jax.numpy as jnp
from jax import lax
from jax.experimental import pallas as pl
from jax.experimental.pallas import tpu as pltpu
from jax.sharding import PartitionSpec as P

very_low = -1e30
norm_eps = 1e-06
pack = 8
f32 = jnp.float32
bf16 = jnp.bfloat16
MESH = pl.DeviceIdType.MESH


def iota(shape, axis):
    return lax.broadcasted_iota(jnp.int32, shape, axis)


def dot(a, b, contract=((1,), (0,))):
    return lax.dot_general(a, b, (contract, ((), ())), preferred_element_type=f32)


def split(x, parts):
    pieces = []
    for _ in range(parts):
        piece = x.astype(bf16)
        pieces.append(piece)
        x = x - piece.astype(f32)
    return pieces


def to_row(column):
    n = column.shape[0]
    eye = iota((n, n), 0) == iota((n, n), 1)
    return jnp.sum(jnp.where(eye, column, 0.0), axis=0, keepdims=True)


def to_column(row):
    n = row.shape[1]
    eye = iota((n, n), 0) == iota((n, n), 1)
    return jnp.sum(jnp.where(eye, row, 0.0), axis=1, keepdims=True)


def unit_rows(matrix):
    total = jnp.sum(matrix * matrix, axis=1, keepdims=True)
    return (matrix * lax.rsqrt(total + norm_eps)).astype(bf16)


def step_kernel(
    dims,
    lengths_ref,
    owner_ref,
    slot_ref,
    probe_ref,
    text_ref,
    labels_ref,
    scale_ref,
    bias_ref,
    tokens_hbm,
    base_hbm,
    value_hbm,
    out_hbm,
    embed_ref,
    image_grad_ref,
    text_grad_ref,
    tokens,
    base,
    value,
    outw,
    probe_wide,
    crop_key,
    base_key,
    len_rows,
    mixed,
    peak_rows,
    total_rows,
    shares,
    base_sum,
    send,
    recv,
    text_all,
    image_all,
    load_sem,
    text_send,
    text_recv,
    crop_send,
    crop_recv,
    image_send,
    image_recv,
):
    owners, loops, cap = dims
    crops, crop_tok, width = tokens.shape
    images, base_tok, _ = base.shape
    heads = probe_ref.shape[1]
    head_dim = width // heads
    lanes = heads * pack
    crop_groups = crops // pack
    base_groups = images // pack
    wide = shares.shape[1]
    slots = owners * cap
    me = lax.axis_index("dp")
    my_loop = lax.axis_index("loop")

    barrier = pltpu.get_barrier_semaphore()
    for k in range(1, owners):
        pl.semaphore_signal(
            barrier, inc=1, device_id=(lax.rem(me + k, owners), my_loop), device_id_type=MESH
        )
    for k in range(1, loops):
        pl.semaphore_signal(
            barrier, inc=1, device_id=(me, lax.rem(my_loop + k, loops)), device_id_type=MESH
        )

    def load_crops(g):
        part = pl.ds(g * pack, pack)
        return pltpu.make_async_copy(tokens_hbm.at[part], tokens.at[part], load_sem.at[g])

    load_value = pltpu.make_async_copy(value_hbm, value, load_sem.at[crop_groups])
    load_base = pltpu.make_async_copy(base_hbm, base, load_sem.at[crop_groups + 1])
    load_out = pltpu.make_async_copy(out_hbm, outw, load_sem.at[crop_groups + 2])
    for g in range(crop_groups):
        load_crops(g).start()
    load_value.start()
    load_base.start()
    load_out.start()

    spread = (iota((heads, lanes), 1) // pack == iota((heads, lanes), 0)).astype(bf16)
    probe_wide[...] = dot(probe_ref[...], spread).astype(bf16)
    lane_of = iota((1, lanes), 1) % pack
    row = iota((pack * crop_tok, lanes), 0)
    crop_key[...] = jnp.where(row // crop_tok == lane_of, row % crop_tok, 2 * crop_tok)
    row = iota((pack * base_tok, lanes), 0)
    base_key[...] = jnp.where(row // base_tok == lane_of, 0, 2)
    lengths = lengths_ref[...].astype(f32)
    of_group = iota((crop_groups, crops), 1) // pack == iota((crop_groups, crops), 0)
    to_lane = (iota((crops, lanes), 0) % pack == iota((crops, lanes), 1) % pack).astype(bf16)
    len_rows[...] = dot(jnp.where(of_group, lengths, 0.0).astype(bf16), to_lane).astype(jnp.int32)

    text_unit = unit_rows(text_ref[...].astype(f32))
    labels = labels_ref[...].astype(f32)
    label_block = jnp.broadcast_to(to_column(labels), (images, wide - width)).astype(bf16)
    text_all[my_loop, :, :width] = text_unit
    text_all[my_loop, :, width:] = label_block

    pl.semaphore_wait(barrier, owners - 1 + loops - 1)

    def share_loop(buffer, send_sem, recv_sem):
        copies = []
        for k in range(1, loops):
            copy = pltpu.make_async_remote_copy(
                src_ref=buffer.at[my_loop],
                dst_ref=buffer.at[my_loop],
                send_sem=send_sem.at[k],
                recv_sem=recv_sem.at[k],
                device_id=(me, lax.rem(my_loop + k, loops)),
                device_id_type=MESH,
            )
            copy.start()
            copies.append(copy)
        return copies

    def await_loop(buffer, send_sem, recv_sem):
        for k in range(1, loops):
            source = lax.rem(my_loop + loops - k, loops)
            pltpu.make_async_remote_copy(
                src_ref=buffer.at[source],
                dst_ref=buffer.at[source],
                send_sem=send_sem.at[k],
                recv_sem=recv_sem.at[k],
                device_id=(me, source),
                device_id_type=MESH,
            ).wait_recv()

    text_copies = share_loop(text_all, text_send, text_recv)

    def pool_group(rows, valid, place):
        scores = dot(rows, probe_wide[...]) * (1.0 / math.sqrt(head_dim))
        masked = jnp.where(valid, scores, very_low)
        peak = jnp.max(masked, axis=0, keepdims=True)
        weight = jnp.exp(masked - peak)
        total = jnp.sum(weight, axis=0, keepdims=True)
        part = pl.ds(place, pack)
        peak_rows[part, :] = jnp.broadcast_to(peak, (pack, lanes))
        total_rows[part, :] = jnp.broadcast_to(total, (pack, lanes))
        summed = dot(weight.astype(bf16), rows, ((0,), (0,)))
        return summed.reshape(heads, pack, width)

    def crop_pair(i, carry):
        found = []
        for half in range(2):
            g = 2 * i + half
            load_crops(g).wait()
            rows = tokens[pl.ds(g * pack, pack)].reshape(pack * crop_tok, width)
            valid = crop_key[...] < len_rows[pl.ds(g, 1), :]
            found.append(pool_group(rows, valid, pl.multiple_of(g * pack, pack)))
        place = pl.ds(pl.multiple_of(i * 2 * pack, 2 * pack), 2 * pack)
        mixed[:, place, :] = jnp.concatenate(found, axis=1).astype(bf16)
        return carry

    lax.fori_loop(0, crop_groups // 2, crop_pair, 0)

    def project(first, count, store):
        for c0 in range(0, width, 256):
            w = min(256, width - c0)
            h0, h1 = c0 // head_dim, (c0 + w - 1) // head_dim + 1
            rows = mixed[h0:h1, first : first + count, :].reshape((h1 - h0) * count, width)
            block = dot(rows, value[:, c0 : c0 + w]).reshape(h1 - h0, count, w)
            head_of = (iota((1, w), 1) + c0) // head_dim
            kept = jnp.where(head_of == h0, block[0], 0.0)
            for h in range(h0 + 1, h1):
                kept = jnp.where(head_of == h, block[h - h0], kept)
            store(c0, w, kept)

    def store_crop(c0, w, block):
        shares[:, c0 : c0 + w] = block.astype(bf16)

    def store_base(c0, w, block):
        base_sum[:, c0 : c0 + w] = block

    load_value.wait()
    project(0, crops, store_crop)

    def by_crop(rows_ref, first, count):
        keep = iota((count, lanes), 0) % pack == iota((count, lanes), 1) % pack
        return jnp.where(keep, rows_ref[first : first + count, :], 0.0)

    meta_width = wide - width
    pieces = split(by_crop(peak_rows, 0, crops), 3) + split(by_crop(total_rows, 0, crops), 3)
    n_pieces = len(pieces)
    k_index = iota((n_pieces * lanes, meta_width), 0)
    gather = k_index // lanes * heads + k_index % lanes // pack == iota(
        (n_pieces * lanes, meta_width), 1
    )
    meta = dot(jnp.concatenate(pieces, axis=1), gather.astype(bf16))
    slot_column = to_column(slot_ref[...].astype(f32))
    meta_lane = iota((crops, meta_width), 1)
    meta = jnp.where(meta_lane == n_pieces * heads, slot_column + 1.0, meta)
    shares[:, width:] = meta.astype(bf16)

    owner_column = owner_ref[...].astype(f32)
    owner_row = to_row(owner_column)
    earlier = (owner_column == owner_row) & (iota((crops, crops), 0) < iota((crops, crops), 1))
    rank = jnp.sum(jnp.where(earlier, 1.0, 0.0), axis=0, keepdims=True)
    target = (owner_row * cap + rank).astype(jnp.int32)
    chosen = (iota((slots, crops), 0) == target).astype(bf16)
    send[...] = dot(chosen, shares[...]).astype(bf16).reshape(owners, cap, wide)

    crop_copies = []
    for k in range(1, owners):
        peer = lax.rem(me + k, owners)
        copy = pltpu.make_async_remote_copy(
            src_ref=send.at[peer],
            dst_ref=recv.at[me],
            send_sem=crop_send.at[k],
            recv_sem=crop_recv.at[k],
            device_id=(peer, my_loop),
            device_id_type=MESH,
        )
        copy.start()
        crop_copies.append(copy)
    recv[me] = send[me]

    load_base.wait()

    def base_pair(i, carry):
        found = []
        for half in range(2):
            g = 2 * i + half
            rows = base[pl.ds(g * pack, pack)].reshape(pack * base_tok, width)
            place = pl.multiple_of(crops + g * pack, pack)
            found.append(pool_group(rows, base_key[...] < 1, place))
        place = pl.ds(pl.multiple_of(crops + i * 2 * pack, 2 * pack), 2 * pack)
        mixed[:, place, :] = jnp.concatenate(found, axis=1).astype(bf16)
        return carry

    lax.fori_loop(0, base_groups // 2, base_pair, 0)
    project(crops, images, store_base)
    fold = (iota((lanes, heads), 0) // pack == iota((lanes, heads), 1)).astype(bf16)

    def folded(x):
        return sum(dot(piece, fold) for piece in split(x, 3))

    base_peak = folded(by_crop(peak_rows, crops, images))
    base_total = folded(by_crop(total_rows, crops, images))
    load_out.wait()
    await_loop(text_all, text_send, text_recv)

    for k in range(1, owners):
        source = lax.rem(me + owners - k, owners)
        pltpu.make_async_remote_copy(
            src_ref=send.at[source],
            dst_ref=recv.at[source],
            send_sem=crop_send.at[k],
            recv_sem=crop_recv.at[k],
            device_id=(source, my_loop),
            device_id_type=MESH,
        ).wait_recv()

    arrived = recv[...].reshape(slots, wide)
    meta = arrived[:, width:]
    m_row, m_col = iota((meta_width, meta_width), 0), iota((meta_width, meta_width), 1)
    is_peak = (m_row < 3 * heads) & (m_row % heads == m_col)
    is_total = (m_row >= 3 * heads) & (m_row < 6 * heads) & (m_row % heads + heads == m_col)
    is_slot = (m_row == 6 * heads) & (m_col == 2 * heads)
    unpack = (is_peak | is_total | is_slot).astype(bf16)
    unpacked = dot(meta, unpack)
    crop_peak = unpacked[:, :heads]
    crop_total = unpacked[:, heads : 2 * heads]
    slot_at = unpacked[:, 2 * heads : 2 * heads + 1]
    across = dot(unpack, meta, ((0,), (1,)))
    slot_row = across[2 * heads : 2 * heads + 1, :]
    member = slot_at == iota((slots, images), 1).astype(f32) + 1.0
    member_t = slot_row == iota((images, slots), 0).astype(f32) + 1.0
    joint = base_peak
    for h in range(heads):
        best = jnp.max(jnp.where(member_t, across[h : h + 1, :], very_low), axis=1, keepdims=True)
        joint = jnp.where(iota((images, heads), 1) == h, jnp.maximum(joint, best), joint)
    member_b = jnp.where(member, 1.0, 0.0).astype(bf16)
    member_tb = jnp.where(member_t, 1.0, 0.0).astype(bf16)
    joint_at = sum(dot(member_b, piece) for piece in split(joint, 3))
    taken = slot_at > 0.5
    rescale = jnp.exp(jnp.where(taken, crop_peak - joint_at, very_low))
    base_rescale = jnp.exp(base_peak - joint)
    collected = sum(dot(member_tb, piece) for piece in split(crop_total * rescale, 3))
    inverse = 1.0 / (base_total * base_rescale + collected)
    inverse_at = sum(dot(member_b, piece) for piece in split(inverse, 2))
    widen = (iota((heads, width), 1) // head_dim == iota((heads, width), 0)).astype(bf16)
    crop_factor = sum(dot(piece, widen) for piece in split(rescale * inverse_at, 2))
    base_factor = sum(dot(piece, widen) for piece in split(base_rescale * inverse, 2))
    scaled = arrived[:, :width].astype(f32) * crop_factor
    merged = sum(dot(member_tb, piece) for piece in split(scaled, 2))
    pooled = (base_sum[...] * base_factor + merged).astype(bf16)
    features = dot(pooled, outw[...])
    embed_ref[...] = features.astype(bf16)
    image_all[my_loop] = unit_rows(features)
    image_copies = share_loop(image_all, image_send, image_recv)

    scale = scale_ref[0]
    bias = bias_ref[0]
    group = loops * images
    texts = text_all[...].reshape(group, wide)
    group_labels = texts[:, width : width + 1].astype(f32)
    sign = jnp.where(group_labels == labels, 1.0, -1.0)
    texts = texts[:, :width]

    def gradient(others, own):
        logits = scale * dot(others, own, ((1,), (1,))) + bias
        tile = (scale * (-sign / (1.0 + jnp.exp(sign * logits)))).astype(bf16)
        return dot(tile, others, ((0,), (0,)))

    image_grad_ref[...] = gradient(texts, image_all[my_loop])
    await_loop(image_all, image_send, image_recv)
    text_grad_ref[...] = gradient(
        image_all[...].reshape(group, width), text_all[my_loop, :, :width]
    )
    for copy in text_copies + crop_copies + image_copies:
        copy.wait_send()


def per_device(
    crop_tokens,
    crop_lengths,
    crop_owner,
    crop_slot,
    base_tokens,
    key_probe,
    value_weight,
    out_weight,
    text_embed,
    pair_labels,
    logit_scale,
    logit_bias,
):
    owners = lax.axis_size("dp")
    loops = lax.axis_size("loop")
    crops, crop_tok, width = crop_tokens.shape
    images, base_tok, _ = base_tokens.shape
    heads = key_probe.shape[1]
    lanes = heads * pack
    cap = max(2, (2 * crops + owners - 1) // owners)
    cap = -(-cap // 16) * 16
    wide = width + 128
    groups = crops // pack
    vmem = pl.BlockSpec(memory_space=pltpu.VMEM)
    smem = pl.BlockSpec(memory_space=pltpu.SMEM)
    hbm = pl.BlockSpec(memory_space=pl.ANY)
    flops = 2 * (crops * crop_tok + images * base_tok) * width * heads * 2
    flops += 2 * (crops + 2 * images) * width * width
    return pl.pallas_call(
        functools.partial(step_kernel, (owners, loops, cap)),
        out_shape=(
            jax.ShapeDtypeStruct((images, width), bf16),
            jax.ShapeDtypeStruct((images, width), f32),
            jax.ShapeDtypeStruct((images, width), f32),
        ),
        in_specs=[vmem] * 6 + [smem] * 2 + [hbm] * 4,
        out_specs=(vmem, vmem, vmem),
        scratch_shapes=[
            pltpu.VMEM(crop_tokens.shape, bf16),
            pltpu.VMEM(base_tokens.shape, bf16),
            pltpu.VMEM((width, width), bf16),
            pltpu.VMEM((width, width), bf16),
            pltpu.VMEM((width, lanes), bf16),
            pltpu.VMEM((pack * crop_tok, lanes), jnp.int32),
            pltpu.VMEM((pack * base_tok, lanes), jnp.int32),
            pltpu.VMEM((groups, lanes), jnp.int32),
            pltpu.VMEM((heads, crops + images, width), bf16),
            pltpu.VMEM((crops + images, lanes), f32),
            pltpu.VMEM((crops + images, lanes), f32),
            pltpu.VMEM((crops, wide), bf16),
            pltpu.VMEM((images, width), f32),
            pltpu.VMEM((owners, cap, wide), bf16),
            pltpu.VMEM((owners, cap, wide), bf16),
            pltpu.VMEM((loops, images, wide), bf16),
            pltpu.VMEM((loops, images, width), bf16),
            pltpu.SemaphoreType.DMA((groups + 3,)),
            pltpu.SemaphoreType.DMA((loops,)),
            pltpu.SemaphoreType.DMA((loops,)),
            pltpu.SemaphoreType.DMA((owners,)),
            pltpu.SemaphoreType.DMA((owners,)),
            pltpu.SemaphoreType.DMA((loops,)),
            pltpu.SemaphoreType.DMA((loops,)),
        ],
        compiler_params=pltpu.CompilerParams(
            collective_id=0, has_side_effects=True, vmem_limit_bytes=56 * 1024 * 1024
        ),
        cost_estimate=pl.CostEstimate(
            flops=flops, bytes_accessed=17 * 1024 * 1024, transcendentals=0
        ),
        name="contrastive_step",
    )(
        crop_lengths,
        crop_owner,
        crop_slot.reshape(1, crops),
        key_probe,
        text_embed,
        pair_labels.reshape(1, images),
        logit_scale,
        logit_bias,
        crop_tokens,
        base_tokens,
        value_weight,
        out_weight,
    )


def solution(mesh):
    return jax.shard_map(
        per_device,
        mesh=mesh,
        in_specs=(
            P(("dp", "loop"), None, None),
            P(("dp", "loop"), None),
            P(("dp", "loop"), None),
            P(("dp", "loop")),
            P(("dp", "loop"), None, None),
            P(),
            P(),
            P(),
            P(("dp", "loop"), None),
            P(("dp", "loop")),
            P(),
            P(),
        ),
        out_specs=(P(("dp", "loop"), None), P(("dp", "loop"), None), P(("dp", "loop"), None)),
        check_vma=False,
    )
```

```python
import functools
import math

import jax
import jax.numpy as jnp
from jax import lax
from jax.experimental import pallas as pl
from jax.experimental.pallas import tpu as pltpu
from jax.sharding import PartitionSpec as P

very_low = -1e30
norm_eps = 1e-06
pack = 8
f32 = jnp.float32
bf16 = jnp.bfloat16
MESH = pl.DeviceIdType.MESH


def iota(shape, axis):
    return lax.broadcasted_iota(jnp.int32, shape, axis)


def dot(a, b, contract=((1,), (0,))):
    return lax.dot_general(a, b, (contract, ((), ())), preferred_element_type=f32)


def split(x, parts):
    pieces = []
    for _ in range(parts):
        piece = x.astype(bf16)
        pieces.append(piece)
        x = x - piece.astype(f32)
    return pieces


def to_row(column):
    n = column.shape[0]
    eye = iota((n, n), 0) == iota((n, n), 1)
    return jnp.sum(jnp.where(eye, column, 0.0), axis=0, keepdims=True)


def to_column(row):
    n = row.shape[1]
    eye = iota((n, n), 0) == iota((n, n), 1)
    return jnp.sum(jnp.where(eye, row, 0.0), axis=1, keepdims=True)


def unit_rows(matrix):
    total = jnp.sum(matrix * matrix, axis=1, keepdims=True)
    return (matrix * lax.rsqrt(total + norm_eps)).astype(bf16)


def column_chunks(width):
    first = min(256, width)
    middle = max(first, (2 * width // 3) // 256 * 256)
    return [(0, first), (first, middle), (middle, width)]


def step_kernel(
    dims,
    lengths_hbm,
    owner_hbm,
    slot_hbm,
    probe_hbm,
    text_hbm,
    labels_hbm,
    scale_ref,
    bias_ref,
    tokens_hbm,
    base_hbm,
    value_hbm,
    out_hbm,
    embed_ref,
    image_grad_ref,
    text_grad_ref,
    lengths_ref,
    owner_ref,
    slot_ref,
    probe_ref,
    text_ref,
    labels_ref,
    tokens,
    base,
    value,
    outw,
    probe_wide,
    crop_key,
    base_key,
    len_rows,
    mixed,
    peak_rows,
    total_rows,
    shares,
    base_sum,
    crop_factor,
    base_factor,
    meta_send,
    meta_recv,
    send_0,
    send_1,
    send_2,
    recv_0,
    recv_1,
    recv_2,
    text_all,
    image_all,
    load_sem,
    small_sem,
    text_send,
    text_recv,
    crop_send,
    crop_recv,
    image_send,
    image_recv,
):
    owners, loops, cap = dims
    crops, crop_tok, width = tokens.shape
    images, base_tok, _ = base.shape
    heads = probe_ref.shape[0]
    head_dim = width // heads
    lanes = heads * pack
    crop_groups = crops // pack
    base_groups = images // pack
    wide = text_all.shape[2]
    slots = owners * cap
    me = lax.axis_index("dp")
    my_loop = lax.axis_index("loop")

    smalls = [
        pltpu.make_async_copy(source, held, small_sem.at[i])
        for i, (source, held) in enumerate(
            [
                (probe_hbm, probe_ref),
                (lengths_hbm, lengths_ref),
                (text_hbm, text_ref),
                (labels_hbm, labels_ref),
                (owner_hbm, owner_ref),
                (slot_hbm, slot_ref),
            ]
        )
    ]

    barrier = pltpu.get_barrier_semaphore()
    for k in range(1, owners):
        pl.semaphore_signal(
            barrier, inc=1, device_id=(lax.rem(me + k, owners), my_loop), device_id_type=MESH
        )
    for k in range(1, loops):
        pl.semaphore_signal(
            barrier, inc=1, device_id=(me, lax.rem(my_loop + k, loops)), device_id_type=MESH
        )

    def load_crops(g):
        part = pl.ds(g * pack, pack)
        return pltpu.make_async_copy(tokens_hbm.at[part], tokens.at[part], load_sem.at[g])

    load_value = pltpu.make_async_copy(value_hbm, value, load_sem.at[crop_groups])
    load_base = pltpu.make_async_copy(base_hbm, base, load_sem.at[crop_groups + 1])
    load_out = pltpu.make_async_copy(out_hbm, outw, load_sem.at[crop_groups + 2])
    for copy in smalls[:4]:
        copy.start()
    for g in range(crop_groups):
        load_crops(g).start()
    for copy in smalls[4:]:
        copy.start()
    load_value.start()
    load_base.start()
    load_out.start()

    spread = (iota((heads, lanes), 1) // pack == iota((heads, lanes), 0)).astype(bf16)
    lane_of = iota((1, lanes), 1) % pack
    row = iota((pack * crop_tok, lanes), 0)
    crop_key[...] = jnp.where(row // crop_tok == lane_of, row % crop_tok, 2 * crop_tok)
    row = iota((pack * base_tok, lanes), 0)
    base_key[...] = jnp.where(row // base_tok == lane_of, 0, 2)
    for copy in smalls:
        copy.wait()
    probe_wide[...] = dot(probe_ref[...], spread, ((0,), (0,))).astype(bf16)
    lengths = lengths_ref[...].astype(f32)
    of_group = iota((crop_groups, crops), 1) // pack == iota((crop_groups, crops), 0)
    to_lane = (iota((crops, lanes), 0) % pack == iota((crops, lanes), 1) % pack).astype(bf16)
    len_rows[...] = dot(jnp.where(of_group, lengths, 0.0).astype(bf16), to_lane).astype(jnp.int32)

    text_unit = unit_rows(text_ref[...].astype(f32))
    labels = labels_ref[...].astype(f32)
    label_block = jnp.broadcast_to(to_column(labels), (images, wide - width)).astype(bf16)
    text_all[my_loop, :, :width] = text_unit
    text_all[my_loop, :, width:] = label_block

    pl.semaphore_wait(barrier, owners - 1 + loops - 1)

    def share_loop(buffer, send_sem, recv_sem):
        copies = []
        for k in range(1, loops):
            copy = pltpu.make_async_remote_copy(
                src_ref=buffer.at[my_loop],
                dst_ref=buffer.at[my_loop],
                send_sem=send_sem.at[k],
                recv_sem=recv_sem.at[k],
                device_id=(me, lax.rem(my_loop + k, loops)),
                device_id_type=MESH,
            )
            copy.start()
            copies.append(copy)
        return copies

    def await_loop(buffer, send_sem, recv_sem):
        for k in range(1, loops):
            source = lax.rem(my_loop + loops - k, loops)
            pltpu.make_async_remote_copy(
                src_ref=buffer.at[source],
                dst_ref=buffer.at[source],
                send_sem=send_sem.at[k],
                recv_sem=recv_sem.at[k],
                device_id=(me, source),
                device_id_type=MESH,
            ).wait_recv()

    text_copies = share_loop(text_all, text_send, text_recv)

    def pool_pair(pair, valid, places):
        scores = [dot(rows, probe_wide[...]) * (1.0 / math.sqrt(head_dim)) for rows in pair]
        found = []
        for rows, score, keep, place in zip(pair, scores, valid, places):
            masked = jnp.where(keep, score, very_low)
            peak = jnp.max(masked, axis=0, keepdims=True)
            weight = jnp.exp(masked - peak)
            total = jnp.sum(weight, axis=0, keepdims=True)
            part = pl.ds(place, pack)
            peak_rows[part, :] = jnp.broadcast_to(peak, (pack, lanes))
            total_rows[part, :] = jnp.broadcast_to(total, (pack, lanes))
            summed = dot(weight.astype(bf16), rows, ((0,), (0,)))
            found.append(summed.reshape(heads, pack, width))
        return jnp.concatenate(found, axis=1).astype(bf16)

    def crop_pair(i, carry):
        groups = (2 * i, 2 * i + 1)
        for g in groups:
            load_crops(g).wait()
        pair = [tokens[pl.ds(g * pack, pack)].reshape(pack * crop_tok, width) for g in groups]
        valid = [crop_key[...] < len_rows[pl.ds(g, 1), :] for g in groups]
        places = [pl.multiple_of(g * pack, pack) for g in groups]
        place = pl.ds(pl.multiple_of(i * 2 * pack, 2 * pack), 2 * pack)
        mixed[:, place, :] = pool_pair(pair, valid, places)
        return carry

    lax.fori_loop(0, crop_groups // 2, crop_pair, 0)

    def project(first, count, c0, c1, store):
        for b0 in range(c0, c1, 256):
            w = min(256, c1 - b0)
            h0, h1 = b0 // head_dim, (b0 + w - 1) // head_dim + 1
            rows = mixed[h0:h1, first : first + count, :].reshape((h1 - h0) * count, width)
            block = dot(rows, value[:, b0 : b0 + w]).reshape(h1 - h0, count, w)
            head_of = (iota((1, w), 1) + b0) // head_dim
            kept = jnp.where(head_of == h0, block[0], 0.0)
            for h in range(h0 + 1, h1):
                kept = jnp.where(head_of == h, block[h - h0], kept)
            store(b0, w, kept)

    def store_crop(b0, w, block):
        shares[:, b0 : b0 + w] = block.astype(bf16)

    def store_base(b0, w, block):
        base_sum[:, b0 : b0 + w] = block

    def by_crop(rows_ref, first, count):
        keep = iota((count, lanes), 0) % pack == iota((count, lanes), 1) % pack
        return jnp.where(keep, rows_ref[first : first + count, :], 0.0)

    meta_width = wide - width
    pieces = split(by_crop(peak_rows, 0, crops), 3) + split(by_crop(total_rows, 0, crops), 3)
    n_pieces = len(pieces)
    k_index = iota((n_pieces * lanes, meta_width), 0)
    gather = k_index // lanes * heads + k_index % lanes // pack == iota(
        (n_pieces * lanes, meta_width), 1
    )
    meta = dot(jnp.concatenate(pieces, axis=1), gather.astype(bf16))
    slot_column = to_column(slot_ref[...].astype(f32))
    meta_lane = iota((crops, meta_width), 1)
    meta = jnp.where(meta_lane == n_pieces * heads, slot_column + 1.0, meta)

    owner_row = owner_ref[...].astype(f32)
    owner_column = to_column(owner_row)
    earlier = (owner_column == owner_row) & (iota((crops, crops), 0) < iota((crops, crops), 1))
    rank = jnp.sum(jnp.where(earlier, 1.0, 0.0), axis=0, keepdims=True)
    target = (owner_row * cap + rank).astype(jnp.int32)
    chosen = (iota((slots, crops), 0) == target).astype(bf16)

    def crop_copy(n, sent, held, k, peer, place):
        return pltpu.make_async_remote_copy(
            src_ref=sent.at[peer],
            dst_ref=held.at[place],
            send_sem=crop_send.at[n, k],
            recv_sem=crop_recv.at[n, k],
            device_id=(peer, my_loop),
            device_id_type=MESH,
        )

    crop_copies = []

    def share_crops(n, sent, held, rows):
        sent[...] = dot(chosen, rows).astype(bf16).reshape(sent.shape)
        for k in range(1, owners):
            copy = crop_copy(n, sent, held, k, lax.rem(me + k, owners), me)
            copy.start()
            crop_copies.append(copy)
        held[me] = sent[me]

    def await_crops(n, sent, held):
        for k in range(1, owners):
            source = lax.rem(me + owners - k, owners)
            crop_copy(n, sent, held, k, source, source).wait_recv()

    share_crops(0, meta_send, meta_recv, meta.astype(bf16))
    load_value.wait()
    chunks = column_chunks(width)
    buffers = [(send_0, recv_0), (send_1, recv_1), (send_2, recv_2)]
    for n, (c0, c1) in enumerate(chunks):
        project(0, crops, c0, c1, store_crop)
        share_crops(n + 1, *buffers[n], shares[:, c0:c1])

    load_base.wait()

    def base_pair(i, carry):
        groups = (2 * i, 2 * i + 1)
        pair = [base[pl.ds(g * pack, pack)].reshape(pack * base_tok, width) for g in groups]
        places = [pl.multiple_of(crops + g * pack, pack) for g in groups]
        place = pl.ds(pl.multiple_of(crops + i * 2 * pack, 2 * pack), 2 * pack)
        mixed[:, place, :] = pool_pair(pair, [base_key[...] < 1] * 2, places)
        return carry

    lax.fori_loop(0, base_groups // 2, base_pair, 0)
    project(crops, images, 0, width, store_base)
    fold = (iota((lanes, heads), 0) // pack == iota((lanes, heads), 1)).astype(bf16)

    def folded(x):
        return sum(dot(piece, fold) for piece in split(x, 3))

    base_peak = folded(by_crop(peak_rows, crops, images))
    base_total = folded(by_crop(total_rows, crops, images))
    await_crops(0, meta_send, meta_recv)

    meta = meta_recv[...].reshape(slots, meta_width)
    m_row, m_col = iota((meta_width, meta_width), 0), iota((meta_width, meta_width), 1)
    is_peak = (m_row < 3 * heads) & (m_row % heads == m_col)
    is_total = (m_row >= 3 * heads) & (m_row < 6 * heads) & (m_row % heads + heads == m_col)
    is_slot = (m_row == 6 * heads) & (m_col == 2 * heads)
    unpack = (is_peak | is_total | is_slot).astype(bf16)
    unpacked = dot(meta, unpack)
    crop_peak = unpacked[:, :heads]
    crop_total = unpacked[:, heads : 2 * heads]
    slot_at = unpacked[:, 2 * heads : 2 * heads + 1]
    across = dot(unpack, meta, ((0,), (1,)))
    slot_row = across[2 * heads : 2 * heads + 1, :]
    member = slot_at == iota((slots, images), 1).astype(f32) + 1.0
    member_t = slot_row == iota((images, slots), 0).astype(f32) + 1.0
    joint = base_peak
    for h in range(heads):
        best = jnp.max(jnp.where(member_t, across[h : h + 1, :], very_low), axis=1, keepdims=True)
        joint = jnp.where(iota((images, heads), 1) == h, jnp.maximum(joint, best), joint)
    member_b = jnp.where(member, 1.0, 0.0).astype(bf16)
    member_tb = jnp.where(member_t, 1.0, 0.0).astype(bf16)
    joint_at = sum(dot(member_b, piece) for piece in split(joint, 3))
    taken = slot_at > 0.5
    rescale = jnp.exp(jnp.where(taken, crop_peak - joint_at, very_low))
    base_rescale = jnp.exp(base_peak - joint)
    collected = sum(dot(member_tb, piece) for piece in split(crop_total * rescale, 3))
    inverse = 1.0 / (base_total * base_rescale + collected)
    inverse_at = sum(dot(member_b, piece) for piece in split(inverse, 2))
    widen = (iota((heads, width), 1) // head_dim == iota((heads, width), 0)).astype(bf16)
    crop_factor[...] = sum(dot(piece, widen) for piece in split(rescale * inverse_at, 2))
    base_factor[...] = sum(dot(piece, widen) for piece in split(base_rescale * inverse, 2))
    load_out.wait()
    await_loop(text_all, text_send, text_recv)
    features = jnp.zeros((images, width), f32)
    for n, (c0, c1) in enumerate(chunks):
        await_crops(n + 1, *buffers[n])
        arrived = buffers[n][1][...].reshape(slots, c1 - c0).astype(f32)
        scaled = (arrived * crop_factor[:, c0:c1]).astype(bf16)
        pooled = base_sum[:, c0:c1] * base_factor[:, c0:c1] + dot(member_tb, scaled)
        features += dot(pooled.astype(bf16), outw[c0:c1, :])
    embed_ref[...] = features.astype(bf16)
    image_all[my_loop] = unit_rows(features)
    image_copies = share_loop(image_all, image_send, image_recv)

    scale = scale_ref[0]
    bias = bias_ref[0]
    group = loops * images
    texts = text_all[...].reshape(group, wide)
    group_labels = texts[:, width : width + 1].astype(f32)
    sign = jnp.where(group_labels == labels, 1.0, -1.0)
    texts = texts[:, :width]

    def gradient(others, own):
        logits = scale * dot(others, own, ((1,), (1,))) + bias
        tile = (scale * (-sign / (1.0 + jnp.exp(sign * logits)))).astype(bf16)
        return dot(tile, others, ((0,), (0,)))

    image_grad_ref[...] = gradient(texts, image_all[my_loop])
    await_loop(image_all, image_send, image_recv)
    text_grad_ref[...] = gradient(
        image_all[...].reshape(group, width), text_all[my_loop, :, :width]
    )
    for copy in text_copies + crop_copies + image_copies:
        copy.wait_send()


def hand_over(embed, image_grad, text_grad, embed_out, image_out, text_out, sem):
    copies = [
        pltpu.make_async_copy(source, held, sem.at[i])
        for i, (source, held) in enumerate(
            [(image_grad, image_out), (text_grad, text_out), (embed, embed_out)]
        )
    ]
    for copy in copies:
        copy.start()
    for copy in copies:
        copy.wait()


def per_device(
    crop_tokens,
    crop_lengths,
    crop_owner,
    crop_slot,
    base_tokens,
    key_probe,
    value_weight,
    out_weight,
    text_embed,
    pair_labels,
    logit_scale,
    logit_bias,
):
    owners = lax.axis_size("dp")
    loops = lax.axis_size("loop")
    crops, crop_tok, width = crop_tokens.shape
    images, base_tok, _ = base_tokens.shape
    heads = key_probe.shape[1]
    lanes = heads * pack
    cap = max(2, (2 * crops + owners - 1) // owners)
    cap = -(-cap // 16) * 16
    wide = width + 128
    groups = crops // pack
    chunk_buffers = [
        pltpu.VMEM((owners, cap, c1 - c0), bf16) for c0, c1 in column_chunks(width)
    ]
    vmem = pl.BlockSpec(memory_space=pltpu.VMEM)
    smem = pl.BlockSpec(memory_space=pltpu.SMEM)
    hbm = pl.BlockSpec(memory_space=pl.ANY)
    flops = 2 * (crops * crop_tok + images * base_tok) * width * heads * 2
    flops += 2 * (crops + 2 * images) * width * width
    step = pl.pallas_call(
        functools.partial(step_kernel, (owners, loops, cap)),
        out_shape=(
            jax.ShapeDtypeStruct((images, width), bf16),
            jax.ShapeDtypeStruct((images, width), f32),
            jax.ShapeDtypeStruct((images, width), f32),
        ),
        in_specs=[hbm] * 6 + [smem] * 2 + [hbm] * 4,
        out_specs=(vmem, vmem, vmem),
        scratch_shapes=[
            pltpu.VMEM((1, crops), jnp.int32),
            pltpu.VMEM((1, crops), jnp.int32),
            pltpu.VMEM((1, crops), jnp.int32),
            pltpu.VMEM((heads, width), bf16),
            pltpu.VMEM((images, width), bf16),
            pltpu.VMEM((1, images), jnp.int32),
            pltpu.VMEM(crop_tokens.shape, bf16),
            pltpu.VMEM(base_tokens.shape, bf16),
            pltpu.VMEM((width, width), bf16),
            pltpu.VMEM((width, width), bf16),
            pltpu.VMEM((width, lanes), bf16),
            pltpu.VMEM((pack * crop_tok, lanes), jnp.int32),
            pltpu.VMEM((pack * base_tok, lanes), jnp.int32),
            pltpu.VMEM((groups, lanes), jnp.int32),
            pltpu.VMEM((heads, crops + images, width), bf16),
            pltpu.VMEM((crops + images, lanes), f32),
            pltpu.VMEM((crops + images, lanes), f32),
            pltpu.VMEM((crops, width), bf16),
            pltpu.VMEM((images, width), f32),
            pltpu.VMEM((owners * cap, width), f32),
            pltpu.VMEM((images, width), f32),
            pltpu.VMEM((owners, cap, wide - width), bf16),
            pltpu.VMEM((owners, cap, wide - width), bf16),
            *chunk_buffers,
            *chunk_buffers,
            pltpu.VMEM((loops, images, wide), bf16),
            pltpu.VMEM((loops, images, width), bf16),
            pltpu.SemaphoreType.DMA((groups + 3,)),
            pltpu.SemaphoreType.DMA((6,)),
            pltpu.SemaphoreType.DMA((loops,)),
            pltpu.SemaphoreType.DMA((loops,)),
            pltpu.SemaphoreType.DMA((len(chunk_buffers) + 1, owners)),
            pltpu.SemaphoreType.DMA((len(chunk_buffers) + 1, owners)),
            pltpu.SemaphoreType.DMA((loops,)),
            pltpu.SemaphoreType.DMA((loops,)),
        ],
        compiler_params=pltpu.CompilerParams(
            collective_id=0, has_side_effects=True, vmem_limit_bytes=56 * 1024 * 1024
        ),
        cost_estimate=pl.CostEstimate(
            flops=flops, bytes_accessed=17 * 1024 * 1024, transcendentals=0
        ),
        name="contrastive_step",
    )
    results = step(
        crop_lengths,
        crop_owner.reshape(1, crops),
        crop_slot.reshape(1, crops),
        key_probe.T,
        text_embed,
        pair_labels.reshape(1, images),
        logit_scale,
        logit_bias,
        crop_tokens,
        base_tokens,
        value_weight,
        out_weight,
    )
    return pl.pallas_call(
        hand_over,
        out_shape=tuple(jax.ShapeDtypeStruct(r.shape, r.dtype) for r in results),
        in_specs=[hbm] * 3,
        out_specs=(hbm, hbm, hbm),
        scratch_shapes=[pltpu.SemaphoreType.DMA((3,))],
        compiler_params=pltpu.CompilerParams(vmem_limit_bytes=56 * 1024 * 1024),
        name="hand_over",
    )(*results)


def solution(mesh):
    return jax.shard_map(
        per_device,
        mesh=mesh,
        in_specs=(
            P(("dp", "loop"), None, None),
            P(("dp", "loop"), None),
            P(("dp", "loop"), None),
            P(("dp", "loop")),
            P(("dp", "loop"), None, None),
            P(),
            P(),
            P(),
            P(("dp", "loop"), None),
            P(("dp", "loop")),
            P(),
            P(),
        ),
        out_specs=(P(("dp", "loop"), None), P(("dp", "loop"), None), P(("dp", "loop"), None)),
        check_vma=False,
    )
```

```python
import functools
import math

import jax
import jax.numpy as jnp
from jax import lax
from jax.experimental import pallas as pl
from jax.experimental.pallas import tpu as pltpu
from jax.sharding import PartitionSpec as P

very_low = -1e30
norm_eps = 1e-06
pack = 8
f32 = jnp.float32
bf16 = jnp.bfloat16
MESH = pl.DeviceIdType.MESH


def iota(shape, axis):
    return lax.broadcasted_iota(jnp.int32, shape, axis)


def dot(a, b, contract=((1,), (0,))):
    return lax.dot_general(a, b, (contract, ((), ())), preferred_element_type=f32)


def split(x, parts):
    pieces = []
    for _ in range(parts):
        piece = x.astype(bf16)
        pieces.append(piece)
        x = x - piece.astype(f32)
    return pieces


def to_row(column):
    n = column.shape[0]
    eye = iota((n, n), 0) == iota((n, n), 1)
    return jnp.sum(jnp.where(eye, column, 0.0), axis=0, keepdims=True)


def to_column(row):
    n = row.shape[1]
    eye = iota((n, n), 0) == iota((n, n), 1)
    return jnp.sum(jnp.where(eye, row, 0.0), axis=1, keepdims=True)


def unit_rows(matrix):
    total = jnp.sum(matrix * matrix, axis=1, keepdims=True)
    return (matrix * lax.rsqrt(total + norm_eps)).astype(bf16)


def column_chunks(width):
    first = min(256, width)
    middle = max(first, (2 * width // 3) // 256 * 256)
    return [(0, first), (first, middle), (middle, width)]


def step_kernel(
    dims,
    lengths_hbm,
    owner_hbm,
    slot_hbm,
    probe_hbm,
    text_hbm,
    labels_hbm,
    scale_ref,
    bias_ref,
    tokens_hbm,
    base_hbm,
    value_hbm,
    out_hbm,
    embed_ref,
    image_grad_ref,
    text_grad_ref,
    lengths_ref,
    owner_ref,
    slot_ref,
    probe_ref,
    text_ref,
    labels_ref,
    tokens,
    base,
    value,
    outw,
    crop_key,
    len_rows,
    mixed,
    peak_cols,
    total_cols,
    shares,
    base_sum,
    crop_factor,
    base_factor,
    meta_send,
    meta_recv,
    send_0,
    send_1,
    send_2,
    recv_0,
    recv_1,
    recv_2,
    text_all,
    image_all,
    load_sem,
    small_sem,
    text_send,
    text_recv,
    crop_send,
    crop_recv,
    image_send,
    image_recv,
):
    owners, loops, cap = dims
    crops, crop_tok, width = tokens.shape
    images, base_tok, _ = base.shape
    heads = probe_ref.shape[0]
    head_dim = width // heads
    lanes = heads * pack
    crop_groups = crops // pack
    base_groups = images // pack
    wide = text_all.shape[2]
    slots = owners * cap
    me = lax.axis_index("dp")
    my_loop = lax.axis_index("loop")

    smalls = [
        pltpu.make_async_copy(source, held, small_sem.at[i])
        for i, (source, held) in enumerate(
            [
                (probe_hbm, probe_ref),
                (lengths_hbm, lengths_ref),
                (text_hbm, text_ref),
                (labels_hbm, labels_ref),
                (owner_hbm, owner_ref),
                (slot_hbm, slot_ref),
            ]
        )
    ]

    barrier = pltpu.get_barrier_semaphore()
    for k in range(1, owners):
        pl.semaphore_signal(
            barrier, inc=1, device_id=(lax.rem(me + k, owners), my_loop), device_id_type=MESH
        )
    for k in range(1, loops):
        pl.semaphore_signal(
            barrier, inc=1, device_id=(me, lax.rem(my_loop + k, loops)), device_id_type=MESH
        )

    def load_crops(g):
        part = pl.ds(g * pack, pack)
        return pltpu.make_async_copy(tokens_hbm.at[part], tokens.at[part], load_sem.at[g])

    load_value = pltpu.make_async_copy(value_hbm, value, load_sem.at[crop_groups])
    load_base = pltpu.make_async_copy(base_hbm, base, load_sem.at[crop_groups + 1])
    load_out = pltpu.make_async_copy(out_hbm, outw, load_sem.at[crop_groups + 2])
    for copy in smalls[:4]:
        copy.start()
    for g in range(crop_groups):
        load_crops(g).start()
    for copy in smalls[4:]:
        copy.start()
    load_value.start()
    load_base.start()
    load_out.start()

    column = iota((pack, pack * crop_tok), 1)
    mine = iota((pack, pack * crop_tok), 0) == column // crop_tok
    crop_key[...] = jnp.where(mine, column % crop_tok, 2 * crop_tok)
    base_key = iota((pack, pack * base_tok), 0) == iota((pack, pack * base_tok), 1) // base_tok
    for copy in smalls:
        copy.wait()
    len_rows[...] = jnp.broadcast_to(to_column(lengths_ref[...].astype(f32)), len_rows.shape)
    peak_cols[...] = jnp.zeros_like(peak_cols)
    total_cols[...] = jnp.zeros_like(total_cols)

    text_unit = unit_rows(text_ref[...].astype(f32))
    labels = labels_ref[...].astype(f32)
    label_block = jnp.broadcast_to(to_column(labels), (images, wide - width)).astype(bf16)
    text_all[my_loop, :, :width] = text_unit
    text_all[my_loop, :, width:] = label_block

    def share_loop(buffer, send_sem, recv_sem):
        copies = []
        for k in range(1, loops):
            copy = pltpu.make_async_remote_copy(
                src_ref=buffer.at[my_loop],
                dst_ref=buffer.at[my_loop],
                send_sem=send_sem.at[k],
                recv_sem=recv_sem.at[k],
                device_id=(me, lax.rem(my_loop + k, loops)),
                device_id_type=MESH,
            )
            copy.start()
            copies.append(copy)
        return copies

    def await_loop(buffer, send_sem, recv_sem):
        for k in range(1, loops):
            source = lax.rem(my_loop + loops - k, loops)
            pltpu.make_async_remote_copy(
                src_ref=buffer.at[source],
                dst_ref=buffer.at[source],
                send_sem=send_sem.at[k],
                recv_sem=recv_sem.at[k],
                device_id=(me, source),
                device_id_type=MESH,
            ).wait_recv()

    def pool_pair(pair, valid, groups):
        scores = [
            dot(probe_ref[...], rows, ((1,), (1,))) * (1.0 / math.sqrt(head_dim)) for rows in pair
        ]
        found = []
        for rows, score, keep, g in zip(pair, scores, valid, groups):
            shape = (heads,) + keep.shape
            copied = jnp.broadcast_to(score[:, None, :], shape)
            masked = jnp.where(jnp.broadcast_to(keep[None], shape), copied, very_low)
            masked = masked.reshape(lanes, keep.shape[1])
            peak = jnp.max(masked, axis=1, keepdims=True)
            weight = jnp.exp(masked - peak)
            total = jnp.sum(weight, axis=1, keepdims=True)
            at = iota((lanes, lanes), 1) == g
            peak_cols[...] = jnp.where(at, peak, peak_cols[...])
            total_cols[...] = jnp.where(at, total, total_cols[...])
            found.append(dot(weight.astype(bf16), rows).reshape(heads, pack, width))
        return jnp.concatenate(found, axis=1).astype(bf16)

    def crop_pair(i, carry):
        groups = (2 * i, 2 * i + 1)
        for g in groups:
            load_crops(g).wait()
        pair = [tokens[pl.ds(g * pack, pack)].reshape(pack * crop_tok, width) for g in groups]
        valid = []
        for g in groups:
            length = len_rows[pl.ds(pl.multiple_of(g * pack, pack), pack), :]
            valid.append(crop_key[...].astype(f32) < length[:, :1])
        place = pl.ds(pl.multiple_of(i * 2 * pack, 2 * pack), 2 * pack)
        mixed[:, place, :] = pool_pair(pair, valid, groups)
        return carry

    lax.fori_loop(0, crop_groups // 2, crop_pair, 0)
    pl.semaphore_wait(barrier, owners - 1 + loops - 1)

    def project(first, count, c0, c1, store):
        for b0 in range(c0, c1, 256):
            w = min(256, c1 - b0)
            h0, h1 = b0 // head_dim, (b0 + w - 1) // head_dim + 1
            rows = mixed[h0:h1, first : first + count, :].reshape((h1 - h0) * count, width)
            block = dot(rows, value[:, b0 : b0 + w]).reshape(h1 - h0, count, w)
            head_of = (iota((1, w), 1) + b0) // head_dim
            kept = jnp.where(head_of == h0, block[0], 0.0)
            for h in range(h0 + 1, h1):
                kept = jnp.where(head_of == h, block[h - h0], kept)
            store(b0, w, kept)

    def store_crop(b0, w, block):
        shares[:, b0 : b0 + w] = block.astype(bf16)

    def store_base(b0, w, block):
        base_sum[:, b0 : b0 + w] = block

    def by_crop(columns_ref, first, count):
        rows = columns_ref[...].T[first // pack : (first + count) // pack, :]
        rows = jnp.broadcast_to(rows[:, None, :], (count // pack, pack, lanes))
        keep = iota((count, lanes), 0) % pack == iota((count, lanes), 1) % pack
        return jnp.where(keep, rows.reshape(count, lanes), 0.0)

    meta_width = wide - width
    pieces = split(by_crop(peak_cols, 0, crops), 3) + split(by_crop(total_cols, 0, crops), 3)
    n_pieces = len(pieces)
    k_index = iota((n_pieces * lanes, meta_width), 0)
    gather = k_index // lanes * heads + k_index % lanes // pack == iota(
        (n_pieces * lanes, meta_width), 1
    )
    meta = dot(jnp.concatenate(pieces, axis=1), gather.astype(bf16))
    slot_column = to_column(slot_ref[...].astype(f32))
    meta_lane = iota((crops, meta_width), 1)
    meta = jnp.where(meta_lane == n_pieces * heads, slot_column + 1.0, meta)

    owner_row = owner_ref[...].astype(f32)
    owner_column = to_column(owner_row)
    earlier = (owner_column == owner_row) & (iota((crops, crops), 0) < iota((crops, crops), 1))
    rank = jnp.sum(jnp.where(earlier, 1.0, 0.0), axis=0, keepdims=True)
    target = (owner_row * cap + rank).astype(jnp.int32)
    chosen = (iota((slots, crops), 0) == target).astype(bf16)

    def crop_copy(n, sent, held, k, peer, place):
        return pltpu.make_async_remote_copy(
            src_ref=sent.at[peer],
            dst_ref=held.at[place],
            send_sem=crop_send.at[n, k],
            recv_sem=crop_recv.at[n, k],
            device_id=(peer, my_loop),
            device_id_type=MESH,
        )

    crop_copies = []

    def share_crops(n, sent, held, rows):
        sent[...] = dot(chosen, rows).astype(bf16).reshape(sent.shape)
        for k in range(1, owners):
            copy = crop_copy(n, sent, held, k, lax.rem(me + k, owners), me)
            copy.start()
            crop_copies.append(copy)
        held[me] = sent[me]

    def await_crops(n, sent, held):
        for k in range(1, owners):
            source = lax.rem(me + owners - k, owners)
            crop_copy(n, sent, held, k, source, source).wait_recv()

    share_crops(0, meta_send, meta_recv, meta.astype(bf16))
    load_value.wait()
    chunks = column_chunks(width)
    buffers = [(send_0, recv_0), (send_1, recv_1), (send_2, recv_2)]
    for n, (c0, c1) in enumerate(chunks):
        project(0, crops, c0, c1, store_crop)
        share_crops(n + 1, *buffers[n], shares[:, c0:c1])

    text_copies = share_loop(text_all, text_send, text_recv)

    load_base.wait()

    def base_pair(i, carry):
        groups = (2 * i, 2 * i + 1)
        pair = [base[pl.ds(g * pack, pack)].reshape(pack * base_tok, width) for g in groups]
        place = pl.ds(pl.multiple_of(crops + i * 2 * pack, 2 * pack), 2 * pack)
        mixed[:, place, :] = pool_pair(
            pair, [base_key] * 2, [crop_groups + g for g in groups]
        )
        return carry

    lax.fori_loop(0, base_groups // 2, base_pair, 0)
    project(crops, images, 0, width, store_base)
    fold = (iota((lanes, heads), 0) // pack == iota((lanes, heads), 1)).astype(bf16)

    def folded(x):
        return sum(dot(piece, fold) for piece in split(x, 3))

    base_peak = folded(by_crop(peak_cols, crops, images))
    base_total = folded(by_crop(total_cols, crops, images))
    await_crops(0, meta_send, meta_recv)

    meta = meta_recv[...].reshape(slots, meta_width)
    m_row, m_col = iota((meta_width, meta_width), 0), iota((meta_width, meta_width), 1)
    is_peak = (m_row < 3 * heads) & (m_row % heads == m_col)
    is_total = (m_row >= 3 * heads) & (m_row < 6 * heads) & (m_row % heads + heads == m_col)
    is_slot = (m_row == 6 * heads) & (m_col == 2 * heads)
    unpack = (is_peak | is_total | is_slot).astype(bf16)
    unpacked = dot(meta, unpack)
    crop_peak = unpacked[:, :heads]
    crop_total = unpacked[:, heads : 2 * heads]
    slot_at = unpacked[:, 2 * heads : 2 * heads + 1]
    across = dot(unpack, meta, ((0,), (1,)))
    slot_row = across[2 * heads : 2 * heads + 1, :]
    member = slot_at == iota((slots, images), 1).astype(f32) + 1.0
    member_t = slot_row == iota((images, slots), 0).astype(f32) + 1.0
    joint = base_peak
    for h in range(heads):
        best = jnp.max(jnp.where(member_t, across[h : h + 1, :], very_low), axis=1, keepdims=True)
        joint = jnp.where(iota((images, heads), 1) == h, jnp.maximum(joint, best), joint)
    member_b = jnp.where(member, 1.0, 0.0).astype(bf16)
    member_tb = jnp.where(member_t, 1.0, 0.0).astype(bf16)
    joint_at = sum(dot(member_b, piece) for piece in split(joint, 3))
    taken = slot_at > 0.5
    rescale = jnp.exp(jnp.where(taken, crop_peak - joint_at, very_low))
    base_rescale = jnp.exp(base_peak - joint)
    collected = sum(dot(member_tb, piece) for piece in split(crop_total * rescale, 3))
    inverse = 1.0 / (base_total * base_rescale + collected)
    inverse_at = sum(dot(member_b, piece) for piece in split(inverse, 2))
    widen = (iota((heads, width), 1) // head_dim == iota((heads, width), 0)).astype(bf16)
    crop_factor[...] = sum(dot(piece, widen) for piece in split(rescale * inverse_at, 2))
    base_factor[...] = sum(dot(piece, widen) for piece in split(base_rescale * inverse, 2))
    load_out.wait()
    await_loop(text_all, text_send, text_recv)
    features = jnp.zeros((images, width), f32)
    for n, (c0, c1) in enumerate(chunks):
        await_crops(n + 1, *buffers[n])
        arrived = buffers[n][1][...].reshape(slots, c1 - c0).astype(f32)
        scaled = (arrived * crop_factor[:, c0:c1]).astype(bf16)
        pooled = base_sum[:, c0:c1] * base_factor[:, c0:c1] + dot(member_tb, scaled)
        features += dot(pooled.astype(bf16), outw[c0:c1, :])
    embed_ref[...] = features.astype(bf16)
    image_all[my_loop] = unit_rows(features)
    image_copies = share_loop(image_all, image_send, image_recv)

    scale = scale_ref[0]
    bias = bias_ref[0]
    group = loops * images
    texts = text_all[...].reshape(group, wide)
    group_labels = texts[:, width : width + 1].astype(f32)
    sign = jnp.where(group_labels == labels, 1.0, -1.0)
    texts = texts[:, :width]

    def gradient(others, own):
        logits = scale * dot(others, own, ((1,), (1,))) + bias
        tile = (scale * (-sign / (1.0 + jnp.exp(sign * logits)))).astype(bf16)
        return dot(tile, others, ((0,), (0,)))

    image_grad_ref[...] = gradient(texts, image_all[my_loop])
    await_loop(image_all, image_send, image_recv)
    text_grad_ref[...] = gradient(
        image_all[...].reshape(group, width), text_all[my_loop, :, :width]
    )
    for copy in text_copies + crop_copies + image_copies:
        copy.wait_send()


def hand_over(embed, image_grad, text_grad, embed_out, image_out, text_out):
    embed_out[...] = embed[...]
    image_out[...] = image_grad[...]
    text_out[...] = text_grad[...]


def per_device(
    crop_tokens,
    crop_lengths,
    crop_owner,
    crop_slot,
    base_tokens,
    key_probe,
    value_weight,
    out_weight,
    text_embed,
    pair_labels,
    logit_scale,
    logit_bias,
):
    owners = lax.axis_size("dp")
    loops = lax.axis_size("loop")
    crops, crop_tok, width = crop_tokens.shape
    images, base_tok, _ = base_tokens.shape
    heads = key_probe.shape[1]
    lanes = heads * pack
    cap = max(2, (2 * crops + owners - 1) // owners)
    cap = -(-cap // 16) * 16
    wide = width + 128
    groups = crops // pack
    chunk_buffers = [
        pltpu.VMEM((owners, cap, c1 - c0), bf16) for c0, c1 in column_chunks(width)
    ]
    vmem = pl.BlockSpec(memory_space=pltpu.VMEM)
    smem = pl.BlockSpec(memory_space=pltpu.SMEM)
    hbm = pl.BlockSpec(memory_space=pl.ANY)
    flops = 2 * (crops * crop_tok + images * base_tok) * width * heads * 2
    flops += 2 * (crops + 2 * images) * width * width
    step = pl.pallas_call(
        functools.partial(step_kernel, (owners, loops, cap)),
        out_shape=(
            jax.ShapeDtypeStruct((images, width), bf16),
            jax.ShapeDtypeStruct((images, width), f32),
            jax.ShapeDtypeStruct((images, width), f32),
        ),
        in_specs=[hbm] * 6 + [smem] * 2 + [hbm] * 4,
        out_specs=(vmem, vmem, vmem),
        scratch_shapes=[
            pltpu.VMEM((1, crops), jnp.int32),
            pltpu.VMEM((1, crops), jnp.int32),
            pltpu.VMEM((1, crops), jnp.int32),
            pltpu.VMEM((heads, width), bf16),
            pltpu.VMEM((images, width), bf16),
            pltpu.VMEM((1, images), jnp.int32),
            pltpu.VMEM(crop_tokens.shape, bf16),
            pltpu.VMEM(base_tokens.shape, bf16),
            pltpu.VMEM((width, width), bf16),
            pltpu.VMEM((width, width), bf16),
            pltpu.VMEM((pack, pack * crop_tok), jnp.int32),
            pltpu.VMEM((crops, 128), f32),
            pltpu.VMEM((heads, crops + images, width), bf16),
            pltpu.VMEM((lanes, lanes), f32),
            pltpu.VMEM((lanes, lanes), f32),
            pltpu.VMEM((crops, width), bf16),
            pltpu.VMEM((images, width), f32),
            pltpu.VMEM((owners * cap, width), f32),
            pltpu.VMEM((images, width), f32),
            pltpu.VMEM((owners, cap, wide - width), bf16),
            pltpu.VMEM((owners, cap, wide - width), bf16),
            *chunk_buffers,
            *chunk_buffers,
            pltpu.VMEM((loops, images, wide), bf16),
            pltpu.VMEM((loops, images, width), bf16),
            pltpu.SemaphoreType.DMA((groups + 3,)),
            pltpu.SemaphoreType.DMA((6,)),
            pltpu.SemaphoreType.DMA((loops,)),
            pltpu.SemaphoreType.DMA((loops,)),
            pltpu.SemaphoreType.DMA((len(chunk_buffers) + 1, owners)),
            pltpu.SemaphoreType.DMA((len(chunk_buffers) + 1, owners)),
            pltpu.SemaphoreType.DMA((loops,)),
            pltpu.SemaphoreType.DMA((loops,)),
        ],
        compiler_params=pltpu.CompilerParams(
            collective_id=0, has_side_effects=True, vmem_limit_bytes=56 * 1024 * 1024
        ),
        cost_estimate=pl.CostEstimate(
            flops=flops, bytes_accessed=17 * 1024 * 1024, transcendentals=0
        ),
        name="contrastive_step",
    )
    results = step(
        crop_lengths,
        crop_owner.reshape(1, crops),
        crop_slot.reshape(1, crops),
        key_probe.T,
        text_embed,
        pair_labels.reshape(1, images),
        logit_scale,
        logit_bias,
        crop_tokens,
        base_tokens,
        value_weight,
        out_weight,
    )
    return pl.pallas_call(
        hand_over,
        out_shape=tuple(jax.ShapeDtypeStruct(r.shape, r.dtype) for r in results),
        in_specs=[vmem] * 3,
        out_specs=(vmem, vmem, vmem),
        compiler_params=pltpu.CompilerParams(vmem_limit_bytes=56 * 1024 * 1024),
        name="hand_over",
    )(*results)


def solution(mesh):
    return jax.shard_map(
        per_device,
        mesh=mesh,
        in_specs=(
            P(("dp", "loop"), None, None),
            P(("dp", "loop"), None),
            P(("dp", "loop"), None),
            P(("dp", "loop")),
            P(("dp", "loop"), None, None),
            P(),
            P(),
            P(),
            P(("dp", "loop"), None),
            P(("dp", "loop")),
            P(),
            P(),
        ),
        out_specs=(P(("dp", "loop"), None), P(("dp", "loop"), None), P(("dp", "loop"), None)),
        check_vma=False,
    )
```

```python
import functools
import math

import jax
import jax.numpy as jnp
from jax import lax
from jax.experimental import pallas as pl
from jax.experimental.pallas import tpu as pltpu
from jax.sharding import PartitionSpec as P

very_low = -1e30
norm_eps = 1e-06
pack = 8
f32 = jnp.float32
bf16 = jnp.bfloat16
MESH = pl.DeviceIdType.MESH


def iota(shape, axis):
    return lax.broadcasted_iota(jnp.int32, shape, axis)


def dot(a, b, contract=((1,), (0,))):
    return lax.dot_general(a, b, (contract, ((), ())), preferred_element_type=f32)


def split(x, parts):
    pieces = []
    for _ in range(parts):
        piece = x.astype(bf16)
        pieces.append(piece)
        x = x - piece.astype(f32)
    return pieces


def to_row(column):
    n = column.shape[0]
    eye = iota((n, n), 0) == iota((n, n), 1)
    return jnp.sum(jnp.where(eye, column, 0.0), axis=0, keepdims=True)


def to_column(row):
    n = row.shape[1]
    eye = iota((n, n), 0) == iota((n, n), 1)
    return jnp.sum(jnp.where(eye, row, 0.0), axis=1, keepdims=True)


def unit_rows(matrix):
    total = jnp.sum(matrix * matrix, axis=1, keepdims=True)
    return (matrix * lax.rsqrt(total + norm_eps)).astype(bf16)


def column_chunks(width, heads):
    first = (heads // 2) * (width // heads) // 256 * 256
    last = max(first, width - 256)
    return [(0, first), (first, last), (last, width)]


def step_kernel(
    dims,
    lengths_hbm,
    owner_hbm,
    slot_hbm,
    probe_hbm,
    text_hbm,
    labels_hbm,
    scale_ref,
    bias_ref,
    tokens_hbm,
    base_hbm,
    value_hbm,
    out_hbm,
    embed_ref,
    image_grad_ref,
    text_grad_ref,
    lengths_ref,
    owner_ref,
    slot_ref,
    probe_ref,
    text_ref,
    labels_ref,
    tokens,
    base,
    value,
    outw,
    crop_key,
    len_rows,
    mixed,
    peak_cols,
    total_cols,
    shares,
    base_sum,
    crop_factor,
    base_factor,
    meta_send,
    meta_recv,
    send_0,
    send_1,
    send_2,
    recv_0,
    recv_1,
    recv_2,
    text_all,
    pooled_0,
    pooled_1,
    pooled_2,
    weights,
    load_sem,
    small_sem,
    loop_send,
    loop_recv,
    crop_send,
    crop_recv,
):
    owners, loops, cap = dims
    crops, crop_tok, width = tokens.shape
    images, base_tok, _ = base.shape
    heads = probe_ref.shape[0]
    head_dim = width // heads
    lanes = heads * pack
    crop_groups = crops // pack
    base_groups = images // pack
    wide = text_all.shape[2]
    slots = owners * cap
    me = lax.axis_index("dp")
    my_loop = lax.axis_index("loop")

    smalls = [
        pltpu.make_async_copy(source, held, small_sem.at[i])
        for i, (source, held) in enumerate(
            [
                (probe_hbm, probe_ref),
                (lengths_hbm, lengths_ref),
                (text_hbm, text_ref),
                (labels_hbm, labels_ref),
                (owner_hbm, owner_ref),
                (slot_hbm, slot_ref),
            ]
        )
    ]

    barrier = pltpu.get_barrier_semaphore()
    for k in range(1, owners):
        pl.semaphore_signal(
            barrier, inc=1, device_id=(lax.rem(me + k, owners), my_loop), device_id_type=MESH
        )
    for k in range(1, loops):
        pl.semaphore_signal(
            barrier, inc=1, device_id=(me, lax.rem(my_loop + k, loops)), device_id_type=MESH
        )

    def load_crops(g):
        part = pl.ds(g * pack, pack)
        return pltpu.make_async_copy(tokens_hbm.at[part], tokens.at[part], load_sem.at[g])

    load_value = pltpu.make_async_copy(value_hbm, value, load_sem.at[crop_groups])
    load_base = pltpu.make_async_copy(base_hbm, base, load_sem.at[crop_groups + 1])
    load_out = pltpu.make_async_copy(out_hbm, outw, load_sem.at[crop_groups + 2])
    for copy in smalls[:4]:
        copy.start()
    for g in range(crop_groups):
        load_crops(g).start()
    for copy in smalls[4:]:
        copy.start()
    load_value.start()
    load_base.start()
    load_out.start()

    column = iota((pack, pack * crop_tok), 1)
    mine = iota((pack, pack * crop_tok), 0) == column // crop_tok
    crop_key[...] = jnp.where(mine, column % crop_tok, 2 * crop_tok)
    base_key = iota((pack, pack * base_tok), 0) == iota((pack, pack * base_tok), 1) // base_tok
    for copy in smalls:
        copy.wait()
    len_rows[...] = jnp.broadcast_to(to_column(lengths_ref[...].astype(f32)), len_rows.shape)
    peak_cols[...] = jnp.zeros_like(peak_cols)
    total_cols[...] = jnp.zeros_like(total_cols)

    text_unit = unit_rows(text_ref[...].astype(f32))
    labels = labels_ref[...].astype(f32)
    label_block = jnp.broadcast_to(to_column(labels), (images, wide - width)).astype(bf16)
    text_all[my_loop, :, :width] = text_unit
    text_all[my_loop, :, width:] = label_block

    def loop_copy(buffer, send_sem, recv_sem, peer, place):
        return pltpu.make_async_remote_copy(
            src_ref=buffer.at[place],
            dst_ref=buffer.at[place],
            send_sem=send_sem,
            recv_sem=recv_sem,
            device_id=(me, peer),
            device_id_type=MESH,
        )

    loop_copies = []

    def share_loop(n, buffer):
        for k in range(1, loops):
            peer = lax.rem(my_loop + k, loops)
            copy = loop_copy(buffer, loop_send.at[n, k], loop_recv.at[n, k], peer, my_loop)
            copy.start()
            loop_copies.append(copy)

    def await_loop(n, buffer):
        for k in range(1, loops):
            source = lax.rem(my_loop + loops - k, loops)
            loop_copy(buffer, loop_send.at[n, k], loop_recv.at[n, k], source, source).wait_recv()

    def pool_pair(pair, valid, groups):
        scores = [
            dot(probe_ref[...], rows, ((1,), (1,))) * (1.0 / math.sqrt(head_dim)) for rows in pair
        ]
        found = []
        for rows, score, keep, g in zip(pair, scores, valid, groups):
            shape = (heads,) + keep.shape
            copied = jnp.broadcast_to(score[:, None, :], shape)
            masked = jnp.where(jnp.broadcast_to(keep[None], shape), copied, very_low)
            masked = masked.reshape(lanes, keep.shape[1])
            peak = jnp.max(masked, axis=1, keepdims=True)
            weight = jnp.exp(masked - peak)
            total = jnp.sum(weight, axis=1, keepdims=True)
            at = iota((lanes, lanes), 1) == g
            peak_cols[...] = jnp.where(at, peak, peak_cols[...])
            total_cols[...] = jnp.where(at, total, total_cols[...])
            found.append(weight.astype(bf16))
        return found

    def mix_pair(pair, weight, place, h0, h1):
        found = [
            dot(part[h0 * pack : h1 * pack], rows).reshape(h1 - h0, pack, width)
            for part, rows in zip(weight, pair)
        ]
        mixed[h0:h1, place, :] = jnp.concatenate(found, axis=1).astype(bf16)

    half = heads // 2

    def crop_pair(i, carry):
        groups = (2 * i, 2 * i + 1)
        for g in groups:
            load_crops(g).wait()
        pair = [tokens[pl.ds(g * pack, pack)].reshape(pack * crop_tok, width) for g in groups]
        valid = []
        for g in groups:
            length = len_rows[pl.ds(pl.multiple_of(g * pack, pack), pack), :]
            valid.append(crop_key[...].astype(f32) < length[:, :1])
        place = pl.ds(pl.multiple_of(i * 2 * pack, 2 * pack), 2 * pack)
        weight = pool_pair(pair, valid, groups)
        for g, part in zip(groups, weight):
            weights[g] = part[half * pack :]
        mix_pair(pair, weight, place, 0, half)
        return carry

    def crop_pair_rest(i, carry):
        groups = (2 * i, 2 * i + 1)
        pair = [tokens[pl.ds(g * pack, pack)].reshape(pack * crop_tok, width) for g in groups]
        place = pl.ds(pl.multiple_of(i * 2 * pack, 2 * pack), 2 * pack)
        found = [
            dot(weights[g], rows).reshape(heads - half, pack, width)
            for g, rows in zip(groups, pair)
        ]
        mixed[half:, place, :] = jnp.concatenate(found, axis=1).astype(bf16)
        return carry

    lax.fori_loop(0, crop_groups // 2, crop_pair, 0)
    pl.semaphore_wait(barrier, owners - 1 + loops - 1)

    def project(first, count, c0, c1, store):
        for b0 in range(c0, c1, 256):
            w = min(256, c1 - b0)
            h0, h1 = b0 // head_dim, (b0 + w - 1) // head_dim + 1
            rows = mixed[h0:h1, first : first + count, :].reshape((h1 - h0) * count, width)
            block = dot(rows, value[:, b0 : b0 + w]).reshape(h1 - h0, count, w)
            head_of = (iota((1, w), 1) + b0) // head_dim
            kept = jnp.where(head_of == h0, block[0], 0.0)
            for h in range(h0 + 1, h1):
                kept = jnp.where(head_of == h, block[h - h0], kept)
            store(b0, w, kept)

    def store_crop(b0, w, block):
        shares[:, b0 : b0 + w] = block.astype(bf16)

    def store_base(b0, w, block):
        base_sum[:, b0 : b0 + w] = block

    def by_crop(columns_ref, first, count):
        rows = columns_ref[...].T[first // pack : (first + count) // pack, :]
        rows = jnp.broadcast_to(rows[:, None, :], (count // pack, pack, lanes))
        keep = iota((count, lanes), 0) % pack == iota((count, lanes), 1) % pack
        return jnp.where(keep, rows.reshape(count, lanes), 0.0)

    meta_width = wide - width
    pieces = split(by_crop(peak_cols, 0, crops), 3) + split(by_crop(total_cols, 0, crops), 3)
    n_pieces = len(pieces)
    k_index = iota((n_pieces * lanes, meta_width), 0)
    gather = k_index // lanes * heads + k_index % lanes // pack == iota(
        (n_pieces * lanes, meta_width), 1
    )
    meta = dot(jnp.concatenate(pieces, axis=1), gather.astype(bf16))
    slot_column = to_column(slot_ref[...].astype(f32))
    meta_lane = iota((crops, meta_width), 1)
    meta = jnp.where(meta_lane == n_pieces * heads, slot_column + 1.0, meta)

    owner_row = owner_ref[...].astype(f32)
    owner_column = to_column(owner_row)
    earlier = (owner_column == owner_row) & (iota((crops, crops), 0) < iota((crops, crops), 1))
    rank = jnp.sum(jnp.where(earlier, 1.0, 0.0), axis=0, keepdims=True)
    target = (owner_row * cap + rank).astype(jnp.int32)
    chosen = (iota((slots, crops), 0) == target).astype(bf16)

    def crop_copy(n, sent, held, k, peer, place):
        return pltpu.make_async_remote_copy(
            src_ref=sent.at[peer],
            dst_ref=held.at[place],
            send_sem=crop_send.at[n, k],
            recv_sem=crop_recv.at[n, k],
            device_id=(peer, my_loop),
            device_id_type=MESH,
        )

    crop_copies = []

    def share_crops(n, sent, held, rows):
        sent[...] = dot(chosen, rows).astype(bf16).reshape(sent.shape)
        for k in range(1, owners):
            copy = crop_copy(n, sent, held, k, lax.rem(me + k, owners), me)
            copy.start()
            crop_copies.append(copy)
        held[me] = sent[me]

    def await_crops(n, sent, held):
        for k in range(1, owners):
            source = lax.rem(me + owners - k, owners)
            crop_copy(n, sent, held, k, source, source).wait_recv()

    share_crops(0, meta_send, meta_recv, meta.astype(bf16))
    load_value.wait()
    chunks = column_chunks(width, heads)
    buffers = [(send_0, recv_0), (send_1, recv_1), (send_2, recv_2)]
    for n, (c0, c1) in enumerate(chunks):
        if n == 1:
            lax.fori_loop(0, crop_groups // 2, crop_pair_rest, 0)
        project(0, crops, c0, c1, store_crop)
        share_crops(n + 1, *buffers[n], shares[:, c0:c1])

    share_loop(0, text_all)

    load_base.wait()

    def base_pair(i, carry):
        groups = (2 * i, 2 * i + 1)
        pair = [base[pl.ds(g * pack, pack)].reshape(pack * base_tok, width) for g in groups]
        place = pl.ds(pl.multiple_of(crops + i * 2 * pack, 2 * pack), 2 * pack)
        weight = pool_pair(pair, [base_key] * 2, [crop_groups + g for g in groups])
        mix_pair(pair, weight, place, 0, heads)
        return carry

    lax.fori_loop(0, base_groups // 2, base_pair, 0)
    project(crops, images, 0, width, store_base)
    fold = (iota((lanes, heads), 0) // pack == iota((lanes, heads), 1)).astype(bf16)

    def folded(x):
        return sum(dot(piece, fold) for piece in split(x, 3))

    base_peak = folded(by_crop(peak_cols, crops, images))
    base_total = folded(by_crop(total_cols, crops, images))
    await_crops(0, meta_send, meta_recv)

    meta = meta_recv[...].reshape(slots, meta_width)
    m_row, m_col = iota((meta_width, meta_width), 0), iota((meta_width, meta_width), 1)
    is_peak = (m_row < 3 * heads) & (m_row % heads == m_col)
    is_total = (m_row >= 3 * heads) & (m_row < 6 * heads) & (m_row % heads + heads == m_col)
    is_slot = (m_row == 6 * heads) & (m_col == 2 * heads)
    unpack = (is_peak | is_total | is_slot).astype(bf16)
    unpacked = dot(meta, unpack)
    crop_peak = unpacked[:, :heads]
    crop_total = unpacked[:, heads : 2 * heads]
    slot_at = unpacked[:, 2 * heads : 2 * heads + 1]
    across = dot(unpack, meta, ((0,), (1,)))
    slot_row = across[2 * heads : 2 * heads + 1, :]
    member = slot_at == iota((slots, images), 1).astype(f32) + 1.0
    member_t = slot_row == iota((images, slots), 0).astype(f32) + 1.0
    joint = base_peak
    for h in range(heads):
        best = jnp.max(jnp.where(member_t, across[h : h + 1, :], very_low), axis=1, keepdims=True)
        joint = jnp.where(iota((images, heads), 1) == h, jnp.maximum(joint, best), joint)
    member_b = jnp.where(member, 1.0, 0.0).astype(bf16)
    member_tb = jnp.where(member_t, 1.0, 0.0).astype(bf16)
    joint_at = sum(dot(member_b, piece) for piece in split(joint, 3))
    taken = slot_at > 0.5
    rescale = jnp.exp(jnp.where(taken, crop_peak - joint_at, very_low))
    base_rescale = jnp.exp(base_peak - joint)
    collected = sum(dot(member_tb, piece) for piece in split(crop_total * rescale, 3))
    inverse = 1.0 / (base_total * base_rescale + collected)
    inverse_at = sum(dot(member_b, piece) for piece in split(inverse, 2))
    widen = (iota((heads, width), 1) // head_dim == iota((heads, width), 0)).astype(bf16)
    crop_factor[...] = sum(dot(piece, widen) for piece in split(rescale * inverse_at, 2))
    base_factor[...] = sum(dot(piece, widen) for piece in split(base_rescale * inverse, 2))
    load_out.wait()
    gathered = [pooled_0, pooled_1, pooled_2]
    features = jnp.zeros((images, width), f32)
    for n, (c0, c1) in enumerate(chunks):
        await_crops(n + 1, *buffers[n])
        arrived = buffers[n][1][...].reshape(slots, c1 - c0).astype(f32)
        scaled = (arrived * crop_factor[:, c0:c1]).astype(bf16)
        pooled = base_sum[:, c0:c1] * base_factor[:, c0:c1] + dot(member_tb, scaled)
        gathered[n][my_loop] = pooled.astype(bf16)
        share_loop(n + 1, gathered[n])
        features += dot(pooled.astype(bf16), outw[c0:c1, :])
    embed_ref[...] = features.astype(bf16)
    image_unit = unit_rows(features)
    await_loop(0, text_all)

    scale = scale_ref[0]
    bias = bias_ref[0]
    group = loops * images
    texts = text_all[...].reshape(group, wide)
    group_labels = texts[:, width : width + 1].astype(f32)
    sign = jnp.where(group_labels == labels, 1.0, -1.0)
    texts = texts[:, :width]

    def gradient(others, own):
        logits = scale * dot(others, own, ((1,), (1,))) + bias
        tile = (scale * (-sign / (1.0 + jnp.exp(sign * logits)))).astype(bf16)
        return dot(tile, others, ((0,), (0,)))

    image_grad_ref[...] = gradient(texts, image_unit)

    features = jnp.zeros((group, width), f32)
    for n, (c0, c1) in enumerate(chunks):
        await_loop(n + 1, gathered[n])
        features += dot(gathered[n][...].reshape(group, c1 - c0), outw[c0:c1, :])
    text_grad_ref[...] = gradient(unit_rows(features), text_all[my_loop, :, :width])
    for copy in loop_copies + crop_copies:
        copy.wait_send()


def hand_over(embed, image_grad, text_grad, embed_out, image_out, text_out):
    embed_out[...] = embed[...]
    image_out[...] = image_grad[...]
    text_out[...] = text_grad[...]


def per_device(
    crop_tokens,
    crop_lengths,
    crop_owner,
    crop_slot,
    base_tokens,
    key_probe,
    value_weight,
    out_weight,
    text_embed,
    pair_labels,
    logit_scale,
    logit_bias,
):
    owners = lax.axis_size("dp")
    loops = lax.axis_size("loop")
    crops, crop_tok, width = crop_tokens.shape
    images, base_tok, _ = base_tokens.shape
    heads = key_probe.shape[1]
    lanes = heads * pack
    cap = max(2, (2 * crops + owners - 1) // owners)
    cap = -(-cap // 16) * 16
    wide = width + 128
    groups = crops // pack
    chunks = column_chunks(width, heads)
    chunk_buffers = [
        pltpu.VMEM((owners, cap, c1 - c0), bf16) for c0, c1 in chunks
    ]
    vmem = pl.BlockSpec(memory_space=pltpu.VMEM)
    smem = pl.BlockSpec(memory_space=pltpu.SMEM)
    hbm = pl.BlockSpec(memory_space=pl.ANY)
    flops = 2 * (crops * crop_tok + images * base_tok) * width * heads * 2
    flops += 2 * (crops + 2 * images) * width * width
    step = pl.pallas_call(
        functools.partial(step_kernel, (owners, loops, cap)),
        out_shape=(
            jax.ShapeDtypeStruct((images, width), bf16),
            jax.ShapeDtypeStruct((images, width), f32),
            jax.ShapeDtypeStruct((images, width), f32),
        ),
        in_specs=[hbm] * 6 + [smem] * 2 + [hbm] * 4,
        out_specs=(vmem, vmem, vmem),
        scratch_shapes=[
            pltpu.VMEM((1, crops), jnp.int32),
            pltpu.VMEM((1, crops), jnp.int32),
            pltpu.VMEM((1, crops), jnp.int32),
            pltpu.VMEM((heads, width), bf16),
            pltpu.VMEM((images, width), bf16),
            pltpu.VMEM((1, images), jnp.int32),
            pltpu.VMEM(crop_tokens.shape, bf16),
            pltpu.VMEM(base_tokens.shape, bf16),
            pltpu.VMEM((width, width), bf16),
            pltpu.VMEM((width, width), bf16),
            pltpu.VMEM((pack, pack * crop_tok), jnp.int32),
            pltpu.VMEM((crops, 128), f32),
            pltpu.VMEM((heads, crops + images, width), bf16),
            pltpu.VMEM((lanes, lanes), f32),
            pltpu.VMEM((lanes, lanes), f32),
            pltpu.VMEM((crops, width), bf16),
            pltpu.VMEM((images, width), f32),
            pltpu.VMEM((owners * cap, width), f32),
            pltpu.VMEM((images, width), f32),
            pltpu.VMEM((owners, cap, wide - width), bf16),
            pltpu.VMEM((owners, cap, wide - width), bf16),
            *chunk_buffers,
            *chunk_buffers,
            pltpu.VMEM((loops, images, wide), bf16),
            *[pltpu.VMEM((loops, images, c1 - c0), bf16) for c0, c1 in chunks],
            pltpu.VMEM((groups, (heads - heads // 2) * pack, pack * crop_tok), bf16),
            pltpu.SemaphoreType.DMA((groups + 3,)),
            pltpu.SemaphoreType.DMA((6,)),
            pltpu.SemaphoreType.DMA((len(chunks) + 1, loops)),
            pltpu.SemaphoreType.DMA((len(chunks) + 1, loops)),
            pltpu.SemaphoreType.DMA((len(chunks) + 1, owners)),
            pltpu.SemaphoreType.DMA((len(chunks) + 1, owners)),
        ],
        compiler_params=pltpu.CompilerParams(
            collective_id=0, has_side_effects=True, vmem_limit_bytes=56 * 1024 * 1024
        ),
        cost_estimate=pl.CostEstimate(
            flops=flops, bytes_accessed=17 * 1024 * 1024, transcendentals=0
        ),
        name="contrastive_step",
    )
    results = step(
        crop_lengths,
        crop_owner.reshape(1, crops),
        crop_slot.reshape(1, crops),
        key_probe.T,
        text_embed,
        pair_labels.reshape(1, images),
        logit_scale,
        logit_bias,
        crop_tokens,
        base_tokens,
        value_weight,
        out_weight,
    )
    return pl.pallas_call(
        hand_over,
        out_shape=tuple(jax.ShapeDtypeStruct(r.shape, r.dtype) for r in results),
        in_specs=[vmem] * 3,
        out_specs=(vmem, vmem, vmem),
        compiler_params=pltpu.CompilerParams(vmem_limit_bytes=56 * 1024 * 1024),
        name="hand_over",
    )(*results)


def solution(mesh):
    return jax.shard_map(
        per_device,
        mesh=mesh,
        in_specs=(
            P(("dp", "loop"), None, None),
            P(("dp", "loop"), None),
            P(("dp", "loop"), None),
            P(("dp", "loop")),
            P(("dp", "loop"), None, None),
            P(),
            P(),
            P(),
            P(("dp", "loop"), None),
            P(("dp", "loop")),
            P(),
            P(),
        ),
        out_specs=(P(("dp", "loop"), None), P(("dp", "loop"), None), P(("dp", "loop"), None)),
        check_vma=False,
    )
```

```python
import functools
import math

import jax
import jax.numpy as jnp
from jax import lax
from jax.experimental import pallas as pl
from jax.experimental.pallas import tpu as pltpu
from jax.sharding import PartitionSpec as P

very_low = -1e30
norm_eps = 1e-06
pack = 8
f32 = jnp.float32
bf16 = jnp.bfloat16
MESH = pl.DeviceIdType.MESH


def iota(shape, axis):
    return lax.broadcasted_iota(jnp.int32, shape, axis)


def dot(a, b, contract=((1,), (0,))):
    return lax.dot_general(a, b, (contract, ((), ())), preferred_element_type=f32)


def split(x, parts):
    pieces = []
    for _ in range(parts):
        piece = x.astype(bf16)
        pieces.append(piece)
        x = x - piece.astype(f32)
    return pieces


def to_row(column):
    n = column.shape[0]
    eye = iota((n, n), 0) == iota((n, n), 1)
    return jnp.sum(jnp.where(eye, column, 0.0), axis=0, keepdims=True)


def to_column(row):
    n = row.shape[1]
    eye = iota((n, n), 0) == iota((n, n), 1)
    return jnp.sum(jnp.where(eye, row, 0.0), axis=1, keepdims=True)


def unit_rows(matrix):
    total = jnp.sum(matrix * matrix, axis=1, keepdims=True)
    return (matrix * lax.rsqrt(total + norm_eps)).astype(bf16)


def column_chunks(width, heads):
    first = (heads // 2) * (width // heads) // 256 * 256
    last = max(first, width - 256)
    return [(0, first), (first, last), (last, width)]


def step_kernel(
    dims,
    lengths_hbm,
    owner_hbm,
    slot_hbm,
    probe_hbm,
    text_hbm,
    labels_hbm,
    scale_ref,
    bias_ref,
    tokens_hbm,
    base_hbm,
    value_hbm,
    out_hbm,
    embed_ref,
    image_grad_ref,
    text_grad_ref,
    lengths_ref,
    owner_ref,
    slot_ref,
    probe_ref,
    text_ref,
    labels_ref,
    tokens,
    base,
    value,
    outw,
    crop_key,
    len_rows,
    mixed,
    peak_cols,
    total_cols,
    shares,
    base_sum,
    crop_factor,
    base_factor,
    meta_send,
    meta_recv,
    send_0,
    send_1,
    send_2,
    recv_0,
    recv_1,
    recv_2,
    text_all,
    pooled_0,
    pooled_1,
    pooled_2,
    weights,
    load_sem,
    small_sem,
    loop_send,
    loop_recv,
    crop_send,
    crop_recv,
):
    owners, loops, cap = dims
    crops, crop_tok, width = tokens.shape
    images, base_tok, _ = base.shape
    heads = probe_ref.shape[0]
    head_dim = width // heads
    lanes = heads * pack
    crop_groups = crops // pack
    base_groups = images // pack
    wide = text_all.shape[2]
    slots = owners * cap
    me = lax.axis_index("dp")
    my_loop = lax.axis_index("loop")

    smalls = [
        pltpu.make_async_copy(source, held, small_sem.at[i])
        for i, (source, held) in enumerate(
            [
                (probe_hbm, probe_ref),
                (lengths_hbm, lengths_ref),
                (text_hbm, text_ref),
                (labels_hbm, labels_ref),
                (owner_hbm, owner_ref),
                (slot_hbm, slot_ref),
            ]
        )
    ]

    barrier = pltpu.get_barrier_semaphore()
    for k in range(1, owners):
        pl.semaphore_signal(
            barrier, inc=1, device_id=(lax.rem(me + k, owners), my_loop), device_id_type=MESH
        )
    for k in range(1, loops):
        pl.semaphore_signal(
            barrier, inc=1, device_id=(me, lax.rem(my_loop + k, loops)), device_id_type=MESH
        )

    def load_crops(g):
        part = pl.ds(g * pack, pack)
        return pltpu.make_async_copy(tokens_hbm.at[part], tokens.at[part], load_sem.at[g])

    load_value = pltpu.make_async_copy(value_hbm, value, load_sem.at[crop_groups])
    load_base = pltpu.make_async_copy(base_hbm, base, load_sem.at[crop_groups + 1])
    load_out = pltpu.make_async_copy(out_hbm, outw, load_sem.at[crop_groups + 2])
    for copy in smalls[:4]:
        copy.start()
    pairs = crop_groups // 2
    ahead = min(3, pairs)
    for g in range(2 * ahead):
        load_crops(g).start()
    for copy in smalls[4:]:
        copy.start()

    def own_tokens(count):
        place = iota((pack, pack * count), 1) - iota((pack, pack * count), 0) * count
        return place, (place >= 0) & (place < count)

    place, mine = own_tokens(crop_tok)
    crop_key[...] = jnp.where(mine, place, 2 * crop_tok)
    _, base_key = own_tokens(base_tok)
    for copy in smalls:
        copy.wait()
    len_rows[...] = jnp.broadcast_to(to_column(lengths_ref[...].astype(f32)), len_rows.shape)
    peak_cols[...] = jnp.zeros_like(peak_cols)
    total_cols[...] = jnp.zeros_like(total_cols)

    text_unit = unit_rows(text_ref[...].astype(f32))
    labels = labels_ref[...].astype(f32)
    label_block = jnp.broadcast_to(to_column(labels), (images, wide - width)).astype(bf16)
    text_all[my_loop, :, :width] = text_unit
    text_all[my_loop, :, width:] = label_block

    def loop_copy(buffer, send_sem, recv_sem, peer, place):
        return pltpu.make_async_remote_copy(
            src_ref=buffer.at[place],
            dst_ref=buffer.at[place],
            send_sem=send_sem,
            recv_sem=recv_sem,
            device_id=(me, peer),
            device_id_type=MESH,
        )

    def share_loop(n, buffer):
        for k in range(1, loops):
            peer = lax.rem(my_loop + k, loops)
            loop_copy(buffer, loop_send.at[n], loop_recv.at[n], peer, my_loop).start()

    def all_loop(n, buffer):
        others = pl.ds(0, loops - 1)
        peer = lax.rem(my_loop + 1, loops)
        return loop_copy(buffer, loop_send.at[n], loop_recv.at[n], peer, others)

    def pool_pair(pair, valid, groups):
        scores = [
            dot(probe_ref[...], rows, ((1,), (1,))) * (1.0 / math.sqrt(head_dim)) for rows in pair
        ]
        found = []
        for rows, score, keep, g in zip(pair, scores, valid, groups):
            shape = (heads,) + keep.shape
            copied = jnp.broadcast_to(score[:, None, :], shape)
            masked = jnp.where(jnp.broadcast_to(keep[None], shape), copied, very_low)
            masked = masked.reshape(lanes, keep.shape[1])
            peak = jnp.max(masked, axis=1, keepdims=True)
            weight = jnp.exp(masked - peak)
            total = jnp.sum(weight, axis=1, keepdims=True)
            at = iota((lanes, lanes), 1) == g
            peak_cols[...] = jnp.where(at, peak, peak_cols[...])
            total_cols[...] = jnp.where(at, total, total_cols[...])
            found.append(weight.astype(bf16))
        return found

    def mix_pair(pair, weight, place, h0, h1):
        found = [
            dot(part[h0 * pack : h1 * pack], rows).reshape(h1 - h0, pack, width)
            for part, rows in zip(weight, pair)
        ]
        mixed[h0:h1, place, :] = jnp.concatenate(found, axis=1).astype(bf16)

    half = heads // 2

    def crop_pair(i, carry):
        groups = (2 * i, 2 * i + 1)
        for g in groups:
            load_crops(g).wait()

        @pl.when(i + ahead < pairs)
        def _():
            load_crops(2 * (i + ahead)).start()
            load_crops(2 * (i + ahead) + 1).start()

        @pl.when(i == min(1, pairs - 1))
        def _():
            load_value.start()

        @pl.when(i == min(2, pairs - 1))
        def _():
            load_base.start()
            load_out.start()

        pair = [tokens[pl.ds(g * pack, pack)].reshape(pack * crop_tok, width) for g in groups]
        valid = []
        for g in groups:
            length = len_rows[pl.ds(pl.multiple_of(g * pack, pack), pack), :]
            valid.append(crop_key[...].astype(f32) < length[:, :1])
        place = pl.ds(pl.multiple_of(i * 2 * pack, 2 * pack), 2 * pack)
        weight = pool_pair(pair, valid, groups)
        for g, part in zip(groups, weight):
            weights[g] = part[half * pack :]
        mix_pair(pair, weight, place, 0, half)
        return carry

    def crop_pair_rest(i, carry):
        groups = (2 * i, 2 * i + 1)
        pair = [tokens[pl.ds(g * pack, pack)].reshape(pack * crop_tok, width) for g in groups]
        place = pl.ds(pl.multiple_of(i * 2 * pack, 2 * pack), 2 * pack)
        found = [
            dot(weights[g], rows).reshape(heads - half, pack, width)
            for g, rows in zip(groups, pair)
        ]
        mixed[half:, place, :] = jnp.concatenate(found, axis=1).astype(bf16)
        return carry

    lax.fori_loop(0, crop_groups // 2, crop_pair, 0)
    pl.semaphore_wait(barrier, owners - 1 + loops - 1)

    def project(first, count, c0, c1, store):
        for b0 in range(c0, c1, 256):
            w = min(256, c1 - b0)
            h0, h1 = b0 // head_dim, (b0 + w - 1) // head_dim + 1
            rows = mixed[h0:h1, first : first + count, :].reshape((h1 - h0) * count, width)
            block = dot(rows, value[:, b0 : b0 + w]).reshape(h1 - h0, count, w)
            column = iota((1, w), 1) + b0
            kept = block[0]
            for h in range(h0 + 1, h1):
                kept = jnp.where(column >= h * head_dim, block[h - h0], kept)
            store(b0, w, kept)

    def store_crop(b0, w, block):
        shares[:, b0 : b0 + w] = block.astype(bf16)

    def store_base(b0, w, block):
        base_sum[:, b0 : b0 + w] = block

    def by_crop(columns_ref, first, count):
        rows = columns_ref[...].T[first // pack : (first + count) // pack, :]
        rows = jnp.broadcast_to(rows[:, None, :], (count // pack, pack, lanes))
        keep = (iota((count, lanes), 0) - iota((count, lanes), 1)) & (pack - 1) == 0
        return jnp.where(keep, rows.reshape(count, lanes), 0.0)

    meta_width = wide - width
    pieces = split(by_crop(peak_cols, 0, crops), 3) + split(by_crop(total_cols, 0, crops), 3)
    n_pieces = len(pieces)
    head_row = lax.shift_right_logical(iota((lanes, meta_width), 0), pack.bit_length() - 1)
    to_head = iota((lanes, meta_width), 1) - head_row
    gather = [(to_head == n * heads).astype(bf16) for n in range(n_pieces)]
    meta = dot(jnp.concatenate(pieces, axis=1), jnp.concatenate(gather, axis=0))
    slot_column = to_column(slot_ref[...].astype(f32))
    meta_lane = iota((crops, meta_width), 1)
    meta = jnp.where(meta_lane == n_pieces * heads, slot_column + 1.0, meta)

    owner_row = owner_ref[...].astype(f32)
    owner_column = to_column(owner_row)
    earlier = (owner_column == owner_row) & (iota((crops, crops), 0) < iota((crops, crops), 1))
    rank = jnp.sum(jnp.where(earlier, 1.0, 0.0), axis=0, keepdims=True)
    target = (owner_row * cap + rank).astype(jnp.int32)
    chosen = (iota((slots, crops), 0) == target).astype(bf16)

    def crop_copy(n, sent, held, peer, source, place):
        return pltpu.make_async_remote_copy(
            src_ref=sent.at[source],
            dst_ref=held.at[place],
            send_sem=crop_send.at[n],
            recv_sem=crop_recv.at[n],
            device_id=(peer, my_loop),
            device_id_type=MESH,
        )

    def all_crops(n, sent, held):
        others = pl.ds(0, owners - 1)
        return crop_copy(n, sent, held, lax.rem(me + 1, owners), others, others)

    def share_crops(n, sent, held, rows):
        sent[...] = dot(chosen, rows).astype(bf16).reshape(sent.shape)
        for k in range(1, owners):
            peer = lax.rem(me + k, owners)
            copy = crop_copy(n, sent, held, peer, peer, me)
            copy.start()
        held[me] = sent[me]

    share_crops(0, meta_send, meta_recv, meta.astype(bf16))
    load_value.wait()
    chunks = column_chunks(width, heads)
    buffers = [(send_0, recv_0), (send_1, recv_1), (send_2, recv_2)]
    for n, (c0, c1) in enumerate(chunks):
        if n == 1:
            lax.fori_loop(0, crop_groups // 2, crop_pair_rest, 0)
        project(0, crops, c0, c1, store_crop)
        share_crops(n + 1, *buffers[n], shares[:, c0:c1])

    share_loop(0, text_all)

    load_base.wait()

    def base_pair(i, carry):
        groups = (2 * i, 2 * i + 1)
        pair = [base[pl.ds(g * pack, pack)].reshape(pack * base_tok, width) for g in groups]
        place = pl.ds(pl.multiple_of(crops + i * 2 * pack, 2 * pack), 2 * pack)
        weight = pool_pair(pair, [base_key] * 2, [crop_groups + g for g in groups])
        mix_pair(pair, weight, place, 0, heads)
        return carry

    lax.fori_loop(0, base_groups // 2, base_pair, 0)
    project(crops, images, 0, width, store_base)
    head_row = lax.shift_right_logical(iota((lanes, heads), 0), pack.bit_length() - 1)
    fold = (head_row == iota((lanes, heads), 1)).astype(bf16)

    def folded(x):
        return sum(dot(piece, fold) for piece in split(x, 3))

    base_peak = folded(by_crop(peak_cols, crops, images))
    base_total = folded(by_crop(total_cols, crops, images))
    all_crops(0, meta_send, meta_recv).wait_recv()

    meta = meta_recv[...].reshape(slots, meta_width)
    m_row, m_col = iota((meta_width, meta_width), 0), iota((meta_width, meta_width), 1)
    gap = m_row - m_col
    is_peak = (m_col < heads) & ((gap == 0) | (gap == heads) | (gap == 2 * heads))
    is_total = (gap == 2 * heads) | (gap == 3 * heads) | (gap == 4 * heads)
    is_total = is_total & (m_col >= heads) & (m_col < 2 * heads)
    is_slot = (m_row == 6 * heads) & (m_col == 2 * heads)
    unpack = (is_peak | is_total | is_slot).astype(bf16)
    unpacked = dot(meta, unpack)
    crop_peak = unpacked[:, :heads]
    crop_total = unpacked[:, heads : 2 * heads]
    slot_at = unpacked[:, 2 * heads : 2 * heads + 1]
    across = dot(unpack, meta, ((0,), (1,)))
    slot_row = across[2 * heads : 2 * heads + 1, :]
    member = slot_at == iota((slots, images), 1).astype(f32) + 1.0
    member_t = slot_row == iota((images, slots), 0).astype(f32) + 1.0
    joint = base_peak
    for h in range(heads):
        best = jnp.max(jnp.where(member_t, across[h : h + 1, :], very_low), axis=1, keepdims=True)
        joint = jnp.where(iota((images, heads), 1) == h, jnp.maximum(joint, best), joint)
    member_b = jnp.where(member, 1.0, 0.0).astype(bf16)
    member_tb = jnp.where(member_t, 1.0, 0.0).astype(bf16)
    joint_at = sum(dot(member_b, piece) for piece in split(joint, 3))
    taken = slot_at > 0.5
    rescale = jnp.exp(jnp.where(taken, crop_peak - joint_at, very_low))
    base_rescale = jnp.exp(base_peak - joint)
    collected = sum(dot(member_tb, piece) for piece in split(crop_total * rescale, 3))
    inverse = 1.0 / (base_total * base_rescale + collected)
    inverse_at = sum(dot(member_b, piece) for piece in split(inverse, 2))
    in_head = iota((heads, width), 1) - iota((heads, width), 0) * head_dim
    widen = ((in_head >= 0) & (in_head < head_dim)).astype(bf16)
    crop_factor[...] = sum(dot(piece, widen) for piece in split(rescale * inverse_at, 2))
    base_factor[...] = sum(dot(piece, widen) for piece in split(base_rescale * inverse, 2))
    load_out.wait()
    gathered = [pooled_0, pooled_1, pooled_2]
    features = jnp.zeros((images, width), f32)
    for n, (c0, c1) in enumerate(chunks):
        all_crops(n + 1, *buffers[n]).wait_recv()
        arrived = buffers[n][1][...].reshape(slots, c1 - c0).astype(f32)
        scaled = (arrived * crop_factor[:, c0:c1]).astype(bf16)
        pooled = base_sum[:, c0:c1] * base_factor[:, c0:c1] + dot(member_tb, scaled)
        gathered[n][my_loop] = pooled.astype(bf16)
        share_loop(n + 1, gathered[n])
        features += dot(pooled.astype(bf16), outw[c0:c1, :])
    embed_ref[...] = features.astype(bf16)
    image_unit = unit_rows(features)
    all_loop(0, text_all).wait_recv()

    scale = scale_ref[0]
    bias = bias_ref[0]
    group = loops * images
    texts = text_all[...].reshape(group, wide)
    group_labels = texts[:, width : width + 1].astype(f32)
    sign = jnp.where(group_labels == labels, 1.0, -1.0)
    texts = texts[:, :width]

    def gradient(others, own):
        logits = scale * dot(others, own, ((1,), (1,))) + bias
        tile = (scale * (-sign / (1.0 + jnp.exp(sign * logits)))).astype(bf16)
        return dot(tile, others, ((0,), (0,)))

    image_grad_ref[...] = gradient(texts, image_unit)

    features = jnp.zeros((group, width), f32)
    for n, (c0, c1) in enumerate(chunks):
        all_loop(n + 1, gathered[n]).wait_recv()
        features += dot(gathered[n][...].reshape(group, c1 - c0), outw[c0:c1, :])
    text_grad_ref[...] = gradient(unit_rows(features), text_all[my_loop, :, :width])
    for n, buffer in enumerate([text_all] + gathered):
        all_loop(n, buffer).wait_send()
    for n, (sent, held) in enumerate([(meta_send, meta_recv)] + buffers):
        all_crops(n, sent, held).wait_send()


def hand_over(embed, image_grad, text_grad, embed_out, image_out, text_out):
    embed_out[...] = embed[...]
    image_out[...] = image_grad[...]
    text_out[...] = text_grad[...]


def per_device(
    crop_tokens,
    crop_lengths,
    crop_owner,
    crop_slot,
    base_tokens,
    key_probe,
    value_weight,
    out_weight,
    text_embed,
    pair_labels,
    logit_scale,
    logit_bias,
):
    owners = lax.axis_size("dp")
    loops = lax.axis_size("loop")
    crops, crop_tok, width = crop_tokens.shape
    images, base_tok, _ = base_tokens.shape
    heads = key_probe.shape[1]
    lanes = heads * pack
    cap = max(2, (2 * crops + owners - 1) // owners)
    cap = -(-cap // 16) * 16
    wide = width + 128
    groups = crops // pack
    chunks = column_chunks(width, heads)
    chunk_buffers = [
        pltpu.VMEM((owners, cap, c1 - c0), bf16) for c0, c1 in chunks
    ]
    vmem = pl.BlockSpec(memory_space=pltpu.VMEM)
    smem = pl.BlockSpec(memory_space=pltpu.SMEM)
    hbm = pl.BlockSpec(memory_space=pl.ANY)
    flops = 2 * (crops * crop_tok + images * base_tok) * width * heads * 2
    flops += 2 * (crops + 2 * images) * width * width
    step = pl.pallas_call(
        functools.partial(step_kernel, (owners, loops, cap)),
        out_shape=(
            jax.ShapeDtypeStruct((images, width), bf16),
            jax.ShapeDtypeStruct((images, width), f32),
            jax.ShapeDtypeStruct((images, width), f32),
        ),
        in_specs=[hbm] * 6 + [smem] * 2 + [hbm] * 4,
        out_specs=(vmem, vmem, vmem),
        scratch_shapes=[
            pltpu.VMEM((1, crops), jnp.int32),
            pltpu.VMEM((1, crops), jnp.int32),
            pltpu.VMEM((1, crops), jnp.int32),
            pltpu.VMEM((heads, width), bf16),
            pltpu.VMEM((images, width), bf16),
            pltpu.VMEM((1, images), jnp.int32),
            pltpu.VMEM(crop_tokens.shape, bf16),
            pltpu.VMEM(base_tokens.shape, bf16),
            pltpu.VMEM((width, width), bf16),
            pltpu.VMEM((width, width), bf16),
            pltpu.VMEM((pack, pack * crop_tok), jnp.int32),
            pltpu.VMEM((crops, 128), f32),
            pltpu.VMEM((heads, crops + images, width), bf16),
            pltpu.VMEM((lanes, lanes), f32),
            pltpu.VMEM((lanes, lanes), f32),
            pltpu.VMEM((crops, width), bf16),
            pltpu.VMEM((images, width), f32),
            pltpu.VMEM((owners * cap, width), f32),
            pltpu.VMEM((images, width), f32),
            pltpu.VMEM((owners, cap, wide - width), bf16),
            pltpu.VMEM((owners, cap, wide - width), bf16),
            *chunk_buffers,
            *chunk_buffers,
            pltpu.VMEM((loops, images, wide), bf16),
            *[pltpu.VMEM((loops, images, c1 - c0), bf16) for c0, c1 in chunks],
            pltpu.VMEM((groups, (heads - heads // 2) * pack, pack * crop_tok), bf16),
            pltpu.SemaphoreType.DMA((groups + 3,)),
            pltpu.SemaphoreType.DMA((6,)),
            pltpu.SemaphoreType.DMA((len(chunks) + 1,)),
            pltpu.SemaphoreType.DMA((len(chunks) + 1,)),
            pltpu.SemaphoreType.DMA((len(chunks) + 1,)),
            pltpu.SemaphoreType.DMA((len(chunks) + 1,)),
        ],
        compiler_params=pltpu.CompilerParams(
            collective_id=0, has_side_effects=True, vmem_limit_bytes=56 * 1024 * 1024
        ),
        cost_estimate=pl.CostEstimate(
            flops=flops, bytes_accessed=17 * 1024 * 1024, transcendentals=0
        ),
        name="contrastive_step",
    )
    results = step(
        crop_lengths,
        crop_owner.reshape(1, crops),
        crop_slot.reshape(1, crops),
        key_probe.T,
        text_embed,
        pair_labels.reshape(1, images),
        logit_scale,
        logit_bias,
        crop_tokens,
        base_tokens,
        value_weight,
        out_weight,
    )
    return pl.pallas_call(
        hand_over,
        out_shape=tuple(jax.ShapeDtypeStruct(r.shape, r.dtype) for r in results),
        in_specs=[vmem] * 3,
        out_specs=(vmem, vmem, vmem),
        compiler_params=pltpu.CompilerParams(vmem_limit_bytes=56 * 1024 * 1024),
        name="hand_over",
    )(*results)


def solution(mesh):
    return jax.shard_map(
        per_device,
        mesh=mesh,
        in_specs=(
            P(("dp", "loop"), None, None),
            P(("dp", "loop"), None),
            P(("dp", "loop"), None),
            P(("dp", "loop")),
            P(("dp", "loop"), None, None),
            P(),
            P(),
            P(),
            P(("dp", "loop"), None),
            P(("dp", "loop")),
            P(),
            P(),
        ),
        out_specs=(P(("dp", "loop"), None), P(("dp", "loop"), None), P(("dp", "loop"), None)),
        check_vma=False,
    )
```

```python
import functools
import math

import jax
import jax.numpy as jnp
from jax import lax
from jax.experimental import pallas as pl
from jax.experimental.pallas import tpu as pltpu
from jax.sharding import PartitionSpec as P

very_low = -1e30
norm_eps = 1e-06
pack = 8
f32 = jnp.float32
bf16 = jnp.bfloat16
MESH = pl.DeviceIdType.MESH


def iota(shape, axis):
    return lax.broadcasted_iota(jnp.int32, shape, axis)


def dot(a, b, contract=((1,), (0,))):
    return lax.dot_general(a, b, (contract, ((), ())), preferred_element_type=f32)


def split(x, parts):
    pieces = []
    for _ in range(parts):
        piece = x.astype(bf16)
        pieces.append(piece)
        x = x - piece.astype(f32)
    return pieces


def to_row(column):
    n = column.shape[0]
    eye = iota((n, n), 0) == iota((n, n), 1)
    return jnp.sum(jnp.where(eye, column, 0.0), axis=0, keepdims=True)


def to_column(row):
    n = row.shape[1]
    eye = iota((n, n), 0) == iota((n, n), 1)
    return jnp.sum(jnp.where(eye, row, 0.0), axis=1, keepdims=True)


def unit_rows(matrix):
    total = jnp.sum(matrix * matrix, axis=1, keepdims=True)
    return (matrix * lax.rsqrt(total + norm_eps)).astype(bf16)


def column_chunks(width, heads):
    first = (heads // 2) * (width // heads) // 256 * 256
    last = max(first, width - 256)
    return [(0, first), (first, last), (last, width)]


def step_kernel(
    dims,
    lengths_hbm,
    owner_hbm,
    slot_hbm,
    probe_hbm,
    text_hbm,
    labels_hbm,
    scale_ref,
    bias_ref,
    tokens_hbm,
    base_hbm,
    value_hbm,
    out_hbm,
    embed_ref,
    image_grad_ref,
    text_grad_ref,
    lengths_ref,
    owner_ref,
    slot_ref,
    probe_ref,
    text_ref,
    labels_ref,
    tokens,
    base,
    value,
    outw,
    crop_key,
    len_rows,
    mixed,
    peak_cols,
    total_cols,
    shares,
    base_sum,
    crop_factor,
    base_factor,
    meta_send,
    meta_recv,
    send_0,
    send_1,
    send_2,
    recv_0,
    recv_1,
    recv_2,
    text_all,
    pooled_0,
    pooled_1,
    pooled_2,
    weights,
    gather_all,
    slot_rows,
    chosen,
    unpack,
    widen,
    load_sem,
    small_sem,
    loop_send,
    loop_recv,
    crop_send,
    crop_recv,
):
    owners, loops, cap = dims
    crops, crop_tok, width = tokens.shape
    images, base_tok, _ = base.shape
    heads = probe_ref.shape[0]
    head_dim = width // heads
    lanes = heads * pack
    crop_groups = crops // pack
    base_groups = images // pack
    wide = text_all.shape[2]
    slots = owners * cap
    me = lax.axis_index("dp")
    my_loop = lax.axis_index("loop")

    smalls = [
        pltpu.make_async_copy(source, held, small_sem.at[i])
        for i, (source, held) in enumerate(
            [
                (probe_hbm, probe_ref),
                (lengths_hbm, lengths_ref),
                (text_hbm, text_ref),
                (labels_hbm, labels_ref),
                (owner_hbm, owner_ref),
                (slot_hbm, slot_ref),
            ]
        )
    ]

    barrier = pltpu.get_barrier_semaphore()
    for k in range(1, owners):
        pl.semaphore_signal(
            barrier, inc=1, device_id=(lax.rem(me + k, owners), my_loop), device_id_type=MESH
        )
    for k in range(1, loops):
        pl.semaphore_signal(
            barrier, inc=1, device_id=(me, lax.rem(my_loop + k, loops)), device_id_type=MESH
        )

    def load_crops(g):
        part = pl.ds(g * pack, pack)
        return pltpu.make_async_copy(tokens_hbm.at[part], tokens.at[part], load_sem.at[g])

    load_value = pltpu.make_async_copy(value_hbm, value, load_sem.at[crop_groups])
    load_base = pltpu.make_async_copy(base_hbm, base, load_sem.at[crop_groups + 1])
    load_out = pltpu.make_async_copy(out_hbm, outw, load_sem.at[crop_groups + 2])
    for copy in smalls[:4]:
        copy.start()
    pairs = crop_groups // 2
    ahead = min(3, pairs)
    for g in range(2 * ahead):
        load_crops(g).start()
    for copy in smalls[4:]:
        copy.start()

    def own_tokens(count):
        place = iota((pack, pack * count), 1) - iota((pack, pack * count), 0) * count
        return place, (place >= 0) & (place < count)

    place, mine = own_tokens(crop_tok)
    crop_key[...] = jnp.where(mine, place, 2 * crop_tok)
    _, base_key = own_tokens(base_tok)
    for copy in smalls:
        copy.wait()
    len_rows[...] = jnp.broadcast_to(to_column(lengths_ref[...].astype(f32)), len_rows.shape)
    peak_cols[...] = jnp.zeros_like(peak_cols)
    total_cols[...] = jnp.zeros_like(total_cols)

    n_pieces, meta_width = 6, wide - width
    head_row = lax.shift_right_logical(iota((lanes, meta_width), 0), pack.bit_length() - 1)
    to_head = iota((lanes, meta_width), 1) - head_row
    for n in range(n_pieces):
        gather_all[pl.ds(n * lanes, lanes), :] = (to_head == n * heads).astype(bf16)
    slot_rows[...] = jnp.broadcast_to(to_column(slot_ref[...].astype(f32)) + 1.0, slot_rows.shape)
    owner_row = owner_ref[...].astype(f32)
    owner_column = to_column(owner_row)
    earlier = (owner_column == owner_row) & (iota((crops, crops), 0) < iota((crops, crops), 1))
    rank = jnp.sum(jnp.where(earlier, 1.0, 0.0), axis=0, keepdims=True)
    target = (owner_row * cap + rank).astype(jnp.int32)
    chosen[...] = (iota((slots, crops), 0) == target).astype(bf16)
    m_row, m_col = iota((meta_width, meta_width), 0), iota((meta_width, meta_width), 1)
    gap = m_row - m_col
    is_peak = (m_col < heads) & ((gap == 0) | (gap == heads) | (gap == 2 * heads))
    is_total = (gap == 2 * heads) | (gap == 3 * heads) | (gap == 4 * heads)
    is_total = is_total & (m_col >= heads) & (m_col < 2 * heads)
    is_slot = (m_row == 6 * heads) & (m_col == 2 * heads)
    unpack[...] = (is_peak | is_total | is_slot).astype(bf16)
    in_head = iota((heads, width), 1) - iota((heads, width), 0) * head_dim
    widen[...] = ((in_head >= 0) & (in_head < head_dim)).astype(bf16)

    text_unit = unit_rows(text_ref[...].astype(f32))
    labels = labels_ref[...].astype(f32)
    label_block = jnp.broadcast_to(to_column(labels), (images, wide - width)).astype(bf16)
    text_all[my_loop, :, :width] = text_unit
    text_all[my_loop, :, width:] = label_block

    def loop_copy(buffer, send_sem, recv_sem, peer, place):
        return pltpu.make_async_remote_copy(
            src_ref=buffer.at[place],
            dst_ref=buffer.at[place],
            send_sem=send_sem,
            recv_sem=recv_sem,
            device_id=(me, peer),
            device_id_type=MESH,
        )

    def share_loop(n, buffer):
        for k in range(1, loops):
            peer = lax.rem(my_loop + k, loops)
            loop_copy(buffer, loop_send.at[n], loop_recv.at[n], peer, my_loop).start()

    def all_loop(n, buffer):
        others = pl.ds(0, loops - 1)
        peer = lax.rem(my_loop + 1, loops)
        return loop_copy(buffer, loop_send.at[n], loop_recv.at[n], peer, others)

    def pool_pair(pair, valid, groups):
        scores = [
            dot(probe_ref[...], rows, ((1,), (1,))) * (1.0 / math.sqrt(head_dim)) for rows in pair
        ]
        found = []
        for rows, score, keep, g in zip(pair, scores, valid, groups):
            shape = (heads,) + keep.shape
            copied = jnp.broadcast_to(score[:, None, :], shape)
            masked = jnp.where(jnp.broadcast_to(keep[None], shape), copied, very_low)
            masked = masked.reshape(lanes, keep.shape[1])
            peak = jnp.max(masked, axis=1, keepdims=True)
            weight = jnp.exp(masked - peak)
            total = jnp.sum(weight, axis=1, keepdims=True)
            at = iota((lanes, lanes), 1) == g
            peak_cols[...] = jnp.where(at, peak, peak_cols[...])
            total_cols[...] = jnp.where(at, total, total_cols[...])
            found.append(weight.astype(bf16))
        return found

    def mix_pair(pair, weight, place, h0, h1):
        found = [
            dot(part[h0 * pack : h1 * pack], rows).reshape(h1 - h0, pack, width)
            for part, rows in zip(weight, pair)
        ]
        mixed[h0:h1, place, :] = jnp.concatenate(found, axis=1).astype(bf16)

    half = heads // 2

    def crop_pair(i, carry):
        groups = (2 * i, 2 * i + 1)
        for g in groups:
            load_crops(g).wait()

        @pl.when(i + ahead < pairs)
        def _():
            load_crops(2 * (i + ahead)).start()
            load_crops(2 * (i + ahead) + 1).start()

        @pl.when(i == min(1, pairs - 1))
        def _():
            load_value.start()

        @pl.when(i == min(2, pairs - 1))
        def _():
            load_base.start()
            load_out.start()

        pair = [tokens[pl.ds(g * pack, pack)].reshape(pack * crop_tok, width) for g in groups]
        valid = []
        for g in groups:
            length = len_rows[pl.ds(pl.multiple_of(g * pack, pack), pack), :]
            valid.append(crop_key[...].astype(f32) < length[:, :1])
        place = pl.ds(pl.multiple_of(i * 2 * pack, 2 * pack), 2 * pack)
        weight = pool_pair(pair, valid, groups)
        for g, part in zip(groups, weight):
            weights[g] = part[half * pack :]
        mix_pair(pair, weight, place, 0, half)
        return carry

    def crop_pair_rest(i, carry):
        groups = (2 * i, 2 * i + 1)
        pair = [tokens[pl.ds(g * pack, pack)].reshape(pack * crop_tok, width) for g in groups]
        place = pl.ds(pl.multiple_of(i * 2 * pack, 2 * pack), 2 * pack)
        found = [
            dot(weights[g], rows).reshape(heads - half, pack, width)
            for g, rows in zip(groups, pair)
        ]
        mixed[half:, place, :] = jnp.concatenate(found, axis=1).astype(bf16)
        return carry

    lax.fori_loop(0, crop_groups // 2, crop_pair, 0)
    pl.semaphore_wait(barrier, owners - 1 + loops - 1)

    def project(first, count, c0, c1, store):
        for b0 in range(c0, c1, 256):
            w = min(256, c1 - b0)
            h0, h1 = b0 // head_dim, (b0 + w - 1) // head_dim + 1
            rows = mixed[h0:h1, first : first + count, :].reshape((h1 - h0) * count, width)
            block = dot(rows, value[:, b0 : b0 + w]).reshape(h1 - h0, count, w)
            column = iota((1, w), 1) + b0
            kept = block[0]
            for h in range(h0 + 1, h1):
                kept = jnp.where(column >= h * head_dim, block[h - h0], kept)
            store(b0, w, kept)

    def store_crop(b0, w, block):
        shares[:, b0 : b0 + w] = block.astype(bf16)

    def store_base(b0, w, block):
        base_sum[:, b0 : b0 + w] = block

    def by_crop(columns_ref, first, count):
        rows = columns_ref[...].T[first // pack : (first + count) // pack, :]
        rows = jnp.broadcast_to(rows[:, None, :], (count // pack, pack, lanes))
        keep = (iota((count, lanes), 0) - iota((count, lanes), 1)) & (pack - 1) == 0
        return jnp.where(keep, rows.reshape(count, lanes), 0.0)

    pieces = split(by_crop(peak_cols, 0, crops), 3) + split(by_crop(total_cols, 0, crops), 3)
    meta = dot(jnp.concatenate(pieces, axis=1), gather_all[...])
    meta_lane = iota((crops, meta_width), 1)
    meta = jnp.where(meta_lane == n_pieces * heads, slot_rows[...], meta)


    def crop_copy(n, sent, held, peer, source, place):
        return pltpu.make_async_remote_copy(
            src_ref=sent.at[source],
            dst_ref=held.at[place],
            send_sem=crop_send.at[n],
            recv_sem=crop_recv.at[n],
            device_id=(peer, my_loop),
            device_id_type=MESH,
        )

    def all_crops(n, sent, held):
        others = pl.ds(0, owners - 1)
        return crop_copy(n, sent, held, lax.rem(me + 1, owners), others, others)

    def share_crops(n, sent, held, rows):
        sent[...] = dot(chosen[...], rows).astype(bf16).reshape(sent.shape)
        for k in range(1, owners):
            peer = lax.rem(me + k, owners)
            copy = crop_copy(n, sent, held, peer, peer, me)
            copy.start()
        held[me] = sent[me]

    share_crops(0, meta_send, meta_recv, meta.astype(bf16))
    load_value.wait()
    chunks = column_chunks(width, heads)
    buffers = [(send_0, recv_0), (send_1, recv_1), (send_2, recv_2)]
    for n, (c0, c1) in enumerate(chunks):
        if n == 1:
            lax.fori_loop(0, crop_groups // 2, crop_pair_rest, 0)
        project(0, crops, c0, c1, store_crop)
        share_crops(n + 1, *buffers[n], shares[:, c0:c1])

    share_loop(0, text_all)

    load_base.wait()

    def base_pair(i, carry):
        groups = (2 * i, 2 * i + 1)
        pair = [base[pl.ds(g * pack, pack)].reshape(pack * base_tok, width) for g in groups]
        place = pl.ds(pl.multiple_of(crops + i * 2 * pack, 2 * pack), 2 * pack)
        weight = pool_pair(pair, [base_key] * 2, [crop_groups + g for g in groups])
        mix_pair(pair, weight, place, 0, heads)
        return carry

    lax.fori_loop(0, base_groups // 2, base_pair, 0)
    project(crops, images, 0, width, store_base)
    head_row = lax.shift_right_logical(iota((lanes, heads), 0), pack.bit_length() - 1)
    fold = (head_row == iota((lanes, heads), 1)).astype(bf16)

    def folded(x):
        return sum(dot(piece, fold) for piece in split(x, 3))

    base_peak = folded(by_crop(peak_cols, crops, images))
    base_total = folded(by_crop(total_cols, crops, images))
    all_crops(0, meta_send, meta_recv).wait_recv()

    meta = meta_recv[...].reshape(slots, meta_width)
    unpacked = dot(meta, unpack[...])
    crop_peak = unpacked[:, :heads]
    crop_total = unpacked[:, heads : 2 * heads]
    slot_at = unpacked[:, 2 * heads : 2 * heads + 1]
    across = dot(unpack[...], meta, ((0,), (1,)))
    slot_row = across[2 * heads : 2 * heads + 1, :]
    member = slot_at == iota((slots, images), 1).astype(f32) + 1.0
    member_t = slot_row == iota((images, slots), 0).astype(f32) + 1.0
    joint = base_peak
    for h in range(heads):
        best = jnp.max(jnp.where(member_t, across[h : h + 1, :], very_low), axis=1, keepdims=True)
        joint = jnp.where(iota((images, heads), 1) == h, jnp.maximum(joint, best), joint)
    member_b = jnp.where(member, 1.0, 0.0).astype(bf16)
    member_tb = jnp.where(member_t, 1.0, 0.0).astype(bf16)
    joint_at = sum(dot(member_b, piece) for piece in split(joint, 3))
    taken = slot_at > 0.5
    rescale = jnp.exp(jnp.where(taken, crop_peak - joint_at, very_low))
    base_rescale = jnp.exp(base_peak - joint)
    collected = sum(dot(member_tb, piece) for piece in split(crop_total * rescale, 3))
    inverse = 1.0 / (base_total * base_rescale + collected)
    inverse_at = sum(dot(member_b, piece) for piece in split(inverse, 2))
    crop_factor[...] = sum(dot(piece, widen[...]) for piece in split(rescale * inverse_at, 2))
    base_factor[...] = sum(dot(piece, widen[...]) for piece in split(base_rescale * inverse, 2))
    load_out.wait()
    gathered = [pooled_0, pooled_1, pooled_2]
    features = jnp.zeros((images, width), f32)
    for n, (c0, c1) in enumerate(chunks):
        all_crops(n + 1, *buffers[n]).wait_recv()
        arrived = buffers[n][1][...].reshape(slots, c1 - c0).astype(f32)
        scaled = (arrived * crop_factor[:, c0:c1]).astype(bf16)
        pooled = base_sum[:, c0:c1] * base_factor[:, c0:c1] + dot(member_tb, scaled)
        gathered[n][my_loop] = pooled.astype(bf16)
        share_loop(n + 1, gathered[n])
        features += dot(pooled.astype(bf16), outw[c0:c1, :])
    embed_ref[...] = features.astype(bf16)
    image_unit = unit_rows(features)
    all_loop(0, text_all).wait_recv()

    scale = scale_ref[0]
    bias = bias_ref[0]
    group = loops * images
    texts = text_all[...].reshape(group, wide)
    group_labels = texts[:, width : width + 1].astype(f32)
    sign = jnp.where(group_labels == labels, 1.0, -1.0)
    texts = texts[:, :width]

    def gradient(others, own):
        logits = scale * dot(others, own, ((1,), (1,))) + bias
        tile = (scale * (-sign / (1.0 + jnp.exp(sign * logits)))).astype(bf16)
        return dot(tile, others, ((0,), (0,)))

    image_grad_ref[...] = gradient(texts, image_unit)

    features = jnp.zeros((group, width), f32)
    for n, (c0, c1) in enumerate(chunks):
        all_loop(n + 1, gathered[n]).wait_recv()
        features += dot(gathered[n][...].reshape(group, c1 - c0), outw[c0:c1, :])
    text_grad_ref[...] = gradient(unit_rows(features), text_all[my_loop, :, :width])
    for n, buffer in enumerate([text_all] + gathered):
        all_loop(n, buffer).wait_send()
    for n, (sent, held) in enumerate([(meta_send, meta_recv)] + buffers):
        all_crops(n, sent, held).wait_send()


def hand_over(embed, image_grad, text_grad, embed_out, image_out, text_out, sem):
    copies = [
        pltpu.make_async_copy(source, held, sem.at[i])
        for i, (source, held) in enumerate(
            [(image_grad, image_out), (text_grad, text_out), (embed, embed_out)]
        )
    ]
    for copy in copies:
        copy.start()
    for copy in copies:
        copy.wait()


def per_device(
    crop_tokens,
    crop_lengths,
    crop_owner,
    crop_slot,
    base_tokens,
    key_probe,
    value_weight,
    out_weight,
    text_embed,
    pair_labels,
    logit_scale,
    logit_bias,
):
    owners = lax.axis_size("dp")
    loops = lax.axis_size("loop")
    crops, crop_tok, width = crop_tokens.shape
    images, base_tok, _ = base_tokens.shape
    heads = key_probe.shape[1]
    lanes = heads * pack
    cap = max(2, (2 * crops + owners - 1) // owners)
    cap = -(-cap // 16) * 16
    wide = width + 128
    groups = crops // pack
    chunks = column_chunks(width, heads)
    chunk_buffers = [
        pltpu.VMEM((owners, cap, c1 - c0), bf16) for c0, c1 in chunks
    ]
    vmem = pl.BlockSpec(memory_space=pltpu.VMEM)
    smem = pl.BlockSpec(memory_space=pltpu.SMEM)
    hbm = pl.BlockSpec(memory_space=pl.ANY)
    flops = 2 * (crops * crop_tok + images * base_tok) * width * heads * 2
    flops += 2 * (crops + 2 * images) * width * width
    step = pl.pallas_call(
        functools.partial(step_kernel, (owners, loops, cap)),
        out_shape=(
            pltpu.VMEM((images, width), bf16),
            pltpu.VMEM((images, width), f32),
            pltpu.VMEM((images, width), f32),
        ),
        in_specs=[hbm] * 6 + [smem] * 2 + [hbm] * 4,
        out_specs=(vmem, vmem, vmem),
        scratch_shapes=[
            pltpu.VMEM((1, crops), jnp.int32),
            pltpu.VMEM((1, crops), jnp.int32),
            pltpu.VMEM((1, crops), jnp.int32),
            pltpu.VMEM((heads, width), bf16),
            pltpu.VMEM((images, width), bf16),
            pltpu.VMEM((1, images), jnp.int32),
            pltpu.VMEM(crop_tokens.shape, bf16),
            pltpu.VMEM(base_tokens.shape, bf16),
            pltpu.VMEM((width, width), bf16),
            pltpu.VMEM((width, width), bf16),
            pltpu.VMEM((pack, pack * crop_tok), jnp.int32),
            pltpu.VMEM((crops, 128), f32),
            pltpu.VMEM((heads, crops + images, width), bf16),
            pltpu.VMEM((lanes, lanes), f32),
            pltpu.VMEM((lanes, lanes), f32),
            pltpu.VMEM((crops, width), bf16),
            pltpu.VMEM((images, width), f32),
            pltpu.VMEM((owners * cap, width), f32),
            pltpu.VMEM((images, width), f32),
            pltpu.VMEM((owners, cap, wide - width), bf16),
            pltpu.VMEM((owners, cap, wide - width), bf16),
            *chunk_buffers,
            *chunk_buffers,
            pltpu.VMEM((loops, images, wide), bf16),
            *[pltpu.VMEM((loops, images, c1 - c0), bf16) for c0, c1 in chunks],
            pltpu.VMEM((groups, (heads - heads // 2) * pack, pack * crop_tok), bf16),
            pltpu.VMEM((6 * lanes, wide - width), bf16),
            pltpu.VMEM((crops, wide - width), f32),
            pltpu.VMEM((owners * cap, crops), bf16),
            pltpu.VMEM((wide - width, wide - width), bf16),
            pltpu.VMEM((heads, width), bf16),
            pltpu.SemaphoreType.DMA((groups + 3,)),
            pltpu.SemaphoreType.DMA((6,)),
            pltpu.SemaphoreType.DMA((len(chunks) + 1,)),
            pltpu.SemaphoreType.DMA((len(chunks) + 1,)),
            pltpu.SemaphoreType.DMA((len(chunks) + 1,)),
            pltpu.SemaphoreType.DMA((len(chunks) + 1,)),
        ],
        compiler_params=pltpu.CompilerParams(
            collective_id=0, has_side_effects=True, vmem_limit_bytes=56 * 1024 * 1024
        ),
        cost_estimate=pl.CostEstimate(
            flops=flops, bytes_accessed=17 * 1024 * 1024, transcendentals=0
        ),
        name="contrastive_step",
    )
    results = step(
        crop_lengths,
        crop_owner.reshape(1, crops),
        crop_slot.reshape(1, crops),
        key_probe.T,
        text_embed,
        pair_labels.reshape(1, images),
        logit_scale,
        logit_bias,
        crop_tokens,
        base_tokens,
        value_weight,
        out_weight,
    )
    return pl.pallas_call(
        hand_over,
        out_shape=tuple(jax.ShapeDtypeStruct(r.shape, r.dtype) for r in results),
        in_specs=[vmem] * 3,
        out_specs=(hbm, hbm, hbm),
        scratch_shapes=[pltpu.SemaphoreType.DMA((3,))],
        compiler_params=pltpu.CompilerParams(vmem_limit_bytes=4 * 1024 * 1024),
        name="hand_over",
    )(*results)


def solution(mesh):
    return jax.shard_map(
        per_device,
        mesh=mesh,
        in_specs=(
            P(("dp", "loop"), None, None),
            P(("dp", "loop"), None),
            P(("dp", "loop"), None),
            P(("dp", "loop")),
            P(("dp", "loop"), None, None),
            P(),
            P(),
            P(),
            P(("dp", "loop"), None),
            P(("dp", "loop")),
            P(),
            P(),
        ),
        out_specs=(P(("dp", "loop"), None), P(("dp", "loop"), None), P(("dp", "loop"), None)),
        check_vma=False,
    )
```

```python
import functools
import math

import jax
import jax.numpy as jnp
from jax import lax
from jax.experimental import pallas as pl
from jax.experimental.pallas import tpu as pltpu
from jax.sharding import PartitionSpec as P

very_low = -1e30
norm_eps = 1e-06
pack = 8
f32 = jnp.float32
bf16 = jnp.bfloat16
MESH = pl.DeviceIdType.MESH


def iota(shape, axis):
    return lax.broadcasted_iota(jnp.int32, shape, axis)


def dot(a, b, contract=((1,), (0,))):
    return lax.dot_general(a, b, (contract, ((), ())), preferred_element_type=f32)


def split(x, parts):
    pieces = []
    for _ in range(parts):
        piece = x.astype(bf16)
        pieces.append(piece)
        x = x - piece.astype(f32)
    return pieces


def to_row(column):
    n = column.shape[0]
    eye = iota((n, n), 0) == iota((n, n), 1)
    return jnp.sum(jnp.where(eye, column, 0.0), axis=0, keepdims=True)


def to_column(row):
    n = row.shape[1]
    eye = iota((n, n), 0) == iota((n, n), 1)
    return jnp.sum(jnp.where(eye, row, 0.0), axis=1, keepdims=True)


def unit_rows(matrix):
    total = jnp.sum(matrix * matrix, axis=1, keepdims=True)
    return (matrix * lax.rsqrt(total + norm_eps)).astype(bf16)


def column_chunks(width, heads):
    first = (heads // 2) * (width // heads) // 256 * 256
    last = max(first, width - 256)
    return [(0, first), (first, last), (last, width)]


def step_kernel(
    dims,
    lengths_hbm,
    owner_hbm,
    slot_hbm,
    probe_hbm,
    text_hbm,
    labels_hbm,
    scale_ref,
    bias_ref,
    tokens_hbm,
    base_hbm,
    value_hbm,
    out_hbm,
    embed_ref,
    image_grad_ref,
    text_grad_ref,
    lengths_ref,
    owner_ref,
    slot_ref,
    probe_ref,
    text_ref,
    labels_ref,
    tokens,
    base,
    value,
    outw,
    crop_key,
    len_rows,
    mixed,
    peak_cols,
    total_cols,
    shares,
    base_sum,
    crop_factor,
    base_factor,
    meta_send,
    meta_recv,
    send_0,
    send_1,
    send_2,
    recv_0,
    recv_1,
    recv_2,
    text_all,
    pooled_0,
    pooled_1,
    pooled_2,
    weights,
    gather_all,
    slot_rows,
    chosen,
    unpack,
    widen,
    load_sem,
    small_sem,
    loop_send,
    loop_recv,
    crop_send,
    crop_recv,
):
    owners, loops, cap = dims
    crops, crop_tok, width = tokens.shape
    images, base_tok, _ = base.shape
    heads = probe_ref.shape[0]
    head_dim = width // heads
    lanes = heads * pack
    crop_groups = crops // pack
    base_groups = images // pack
    wide = text_all.shape[2]
    slots = owners * cap
    me = lax.axis_index("dp")
    my_loop = lax.axis_index("loop")

    smalls = [
        pltpu.make_async_copy(source, held, small_sem.at[i])
        for i, (source, held) in enumerate(
            [
                (probe_hbm, probe_ref),
                (lengths_hbm, lengths_ref),
                (text_hbm, text_ref),
                (labels_hbm, labels_ref),
                (owner_hbm, owner_ref),
                (slot_hbm, slot_ref),
            ]
        )
    ]

    def load_crops(g):
        part = pl.ds(g * pack, pack)
        return pltpu.make_async_copy(tokens_hbm.at[part], tokens.at[part], load_sem.at[g])

    load_value = pltpu.make_async_copy(value_hbm, value, load_sem.at[crop_groups])
    load_base = pltpu.make_async_copy(base_hbm, base, load_sem.at[crop_groups + 1])
    load_out = pltpu.make_async_copy(out_hbm, outw, load_sem.at[crop_groups + 2])
    for copy in smalls:
        copy.start()
    pairs = crop_groups // 2
    ahead = min(3, pairs)
    for g in range(2 * ahead):
        load_crops(g).start()
    barrier = pltpu.get_barrier_semaphore()
    for k in range(1, owners):
        pl.semaphore_signal(
            barrier, inc=1, device_id=(lax.rem(me + k, owners), my_loop), device_id_type=MESH
        )
    for k in range(1, loops):
        pl.semaphore_signal(
            barrier, inc=1, device_id=(me, lax.rem(my_loop + k, loops)), device_id_type=MESH
        )

    def own_tokens(count):
        place = iota((pack, pack * count), 1) - iota((pack, pack * count), 0) * count
        return place, (place >= 0) & (place < count)

    place, mine = own_tokens(crop_tok)
    crop_key[...] = jnp.where(mine, place, 2 * crop_tok)
    _, base_key = own_tokens(base_tok)
    for copy in smalls:
        copy.wait()
    len_rows[...] = jnp.broadcast_to(to_column(lengths_ref[...].astype(f32)), len_rows.shape)
    peak_cols[...] = jnp.zeros_like(peak_cols)
    total_cols[...] = jnp.zeros_like(total_cols)

    n_pieces, meta_width = 6, wide - width
    head_row = lax.shift_right_logical(iota((lanes, meta_width), 0), pack.bit_length() - 1)
    to_head = iota((lanes, meta_width), 1) - head_row
    for n in range(n_pieces):
        gather_all[pl.ds(n * lanes, lanes), :] = (to_head == n * heads).astype(bf16)
    slot_rows[...] = jnp.broadcast_to(to_column(slot_ref[...].astype(f32)) + 1.0, slot_rows.shape)
    owner_row = owner_ref[...].astype(f32)
    owner_column = to_column(owner_row)
    earlier = (owner_column == owner_row) & (iota((crops, crops), 0) < iota((crops, crops), 1))
    rank = jnp.sum(jnp.where(earlier, 1.0, 0.0), axis=0, keepdims=True)
    target = (owner_row * cap + rank).astype(jnp.int32)
    chosen[...] = (iota((slots, crops), 0) == target).astype(bf16)
    m_row, m_col = iota((meta_width, meta_width), 0), iota((meta_width, meta_width), 1)
    gap = m_row - m_col
    is_peak = (m_col < heads) & ((gap == 0) | (gap == heads) | (gap == 2 * heads))
    is_total = (gap == 2 * heads) | (gap == 3 * heads) | (gap == 4 * heads)
    is_total = is_total & (m_col >= heads) & (m_col < 2 * heads)
    is_slot = (m_row == 6 * heads) & (m_col == 2 * heads)
    unpack[...] = (is_peak | is_total | is_slot).astype(bf16)
    in_head = iota((heads, width), 1) - iota((heads, width), 0) * head_dim
    widen[...] = ((in_head >= 0) & (in_head < head_dim)).astype(bf16)

    text_unit = unit_rows(text_ref[...].astype(f32))
    labels = labels_ref[...].astype(f32)
    label_block = jnp.broadcast_to(to_column(labels), (images, wide - width)).astype(bf16)
    text_all[my_loop, :, :width] = text_unit
    text_all[my_loop, :, width:] = label_block

    def loop_copy(buffer, send_sem, recv_sem, peer, place):
        return pltpu.make_async_remote_copy(
            src_ref=buffer.at[place],
            dst_ref=buffer.at[place],
            send_sem=send_sem,
            recv_sem=recv_sem,
            device_id=(me, peer),
            device_id_type=MESH,
        )

    def share_loop(n, buffer):
        for k in range(1, loops):
            peer = lax.rem(my_loop + k, loops)
            loop_copy(buffer, loop_send.at[n], loop_recv.at[n], peer, my_loop).start()

    def all_loop(n, buffer):
        others = pl.ds(0, loops - 1)
        peer = lax.rem(my_loop + 1, loops)
        return loop_copy(buffer, loop_send.at[n], loop_recv.at[n], peer, others)

    def pool_pair(pair, valid, groups):
        scores = [
            dot(probe_ref[...], rows, ((1,), (1,))) * (1.0 / math.sqrt(head_dim)) for rows in pair
        ]
        found = []
        for rows, score, keep, g in zip(pair, scores, valid, groups):
            shape = (heads,) + keep.shape
            copied = jnp.broadcast_to(score[:, None, :], shape)
            masked = jnp.where(jnp.broadcast_to(keep[None], shape), copied, very_low)
            masked = masked.reshape(lanes, keep.shape[1])
            peak = jnp.max(masked, axis=1, keepdims=True)
            weight = jnp.exp(masked - peak)
            total = jnp.sum(weight, axis=1, keepdims=True)
            at = iota((lanes, lanes), 1) == g
            peak_cols[...] = jnp.where(at, peak, peak_cols[...])
            total_cols[...] = jnp.where(at, total, total_cols[...])
            found.append(weight.astype(bf16))
        return found

    def mix_pair(pair, weight, place, h0, h1):
        found = [
            dot(part[h0 * pack : h1 * pack], rows).reshape(h1 - h0, pack, width)
            for part, rows in zip(weight, pair)
        ]
        mixed[h0:h1, place, :] = jnp.concatenate(found, axis=1).astype(bf16)

    half = heads // 2

    def crop_pair(i, carry):
        groups = (2 * i, 2 * i + 1)
        for g in groups:
            load_crops(g).wait()

        @pl.when(i + ahead < pairs)
        def _():
            load_crops(2 * (i + ahead)).start()
            load_crops(2 * (i + ahead) + 1).start()

        @pl.when(i == min(1, pairs - 1))
        def _():
            load_value.start()

        @pl.when(i == min(2, pairs - 1))
        def _():
            load_base.start()
            load_out.start()

        pair = [tokens[pl.ds(g * pack, pack)].reshape(pack * crop_tok, width) for g in groups]
        valid = []
        for g in groups:
            length = len_rows[pl.ds(pl.multiple_of(g * pack, pack), pack), :]
            valid.append(crop_key[...].astype(f32) < length[:, :1])
        place = pl.ds(pl.multiple_of(i * 2 * pack, 2 * pack), 2 * pack)
        weight = pool_pair(pair, valid, groups)
        for g, part in zip(groups, weight):
            weights[g] = part[half * pack :]
        mix_pair(pair, weight, place, 0, half)
        return carry

    def crop_pair_rest(i, carry):
        groups = (2 * i, 2 * i + 1)
        pair = [tokens[pl.ds(g * pack, pack)].reshape(pack * crop_tok, width) for g in groups]
        place = pl.ds(pl.multiple_of(i * 2 * pack, 2 * pack), 2 * pack)
        found = [
            dot(weights[g], rows).reshape(heads - half, pack, width)
            for g, rows in zip(groups, pair)
        ]
        mixed[half:, place, :] = jnp.concatenate(found, axis=1).astype(bf16)
        return carry

    lax.fori_loop(0, crop_groups // 2, crop_pair, 0)
    pl.semaphore_wait(barrier, owners - 1 + loops - 1)

    def project(first, count, c0, c1, store):
        for b0 in range(c0, c1, 256):
            w = min(256, c1 - b0)
            h0, h1 = b0 // head_dim, (b0 + w - 1) // head_dim + 1
            rows = mixed[h0:h1, first : first + count, :].reshape((h1 - h0) * count, width)
            block = dot(rows, value[:, b0 : b0 + w]).reshape(h1 - h0, count, w)
            column = iota((1, w), 1) + b0
            kept = block[0]
            for h in range(h0 + 1, h1):
                kept = jnp.where(column >= h * head_dim, block[h - h0], kept)
            store(b0, w, kept)

    def store_crop(b0, w, block):
        shares[:, b0 : b0 + w] = block.astype(bf16)

    def store_base(b0, w, block):
        base_sum[:, b0 : b0 + w] = block

    def by_crop(columns_ref, first, count):
        rows = columns_ref[...].T[first // pack : (first + count) // pack, :]
        rows = jnp.broadcast_to(rows[:, None, :], (count // pack, pack, lanes))
        keep = (iota((count, lanes), 0) - iota((count, lanes), 1)) & (pack - 1) == 0
        return jnp.where(keep, rows.reshape(count, lanes), 0.0)

    pieces = split(by_crop(peak_cols, 0, crops), 3) + split(by_crop(total_cols, 0, crops), 3)
    meta = dot(jnp.concatenate(pieces, axis=1), gather_all[...])
    meta_lane = iota((crops, meta_width), 1)
    meta = jnp.where(meta_lane == n_pieces * heads, slot_rows[...], meta)


    def crop_copy(n, sent, held, peer, source, place):
        return pltpu.make_async_remote_copy(
            src_ref=sent.at[source],
            dst_ref=held.at[place],
            send_sem=crop_send.at[n],
            recv_sem=crop_recv.at[n],
            device_id=(peer, my_loop),
            device_id_type=MESH,
        )

    def all_crops(n, sent, held):
        others = pl.ds(0, owners - 1)
        return crop_copy(n, sent, held, lax.rem(me + 1, owners), others, others)

    def share_crops(n, sent, held, rows):
        sent[...] = dot(chosen[...], rows).astype(bf16).reshape(sent.shape)
        for k in range(1, owners):
            peer = lax.rem(me + k, owners)
            copy = crop_copy(n, sent, held, peer, peer, me)
            copy.start()
        held[me] = sent[me]

    share_crops(0, meta_send, meta_recv, meta.astype(bf16))
    load_value.wait()
    chunks = column_chunks(width, heads)
    buffers = [(send_0, recv_0), (send_1, recv_1), (send_2, recv_2)]
    for n, (c0, c1) in enumerate(chunks):
        if n == 1:
            lax.fori_loop(0, crop_groups // 2, crop_pair_rest, 0)
        project(0, crops, c0, c1, store_crop)
        share_crops(n + 1, *buffers[n], shares[:, c0:c1])

    share_loop(0, text_all)

    load_base.wait()

    def base_pair(i, carry):
        groups = (2 * i, 2 * i + 1)
        pair = [base[pl.ds(g * pack, pack)].reshape(pack * base_tok, width) for g in groups]
        place = pl.ds(pl.multiple_of(crops + i * 2 * pack, 2 * pack), 2 * pack)
        weight = pool_pair(pair, [base_key] * 2, [crop_groups + g for g in groups])
        mix_pair(pair, weight, place, 0, heads)
        return carry

    lax.fori_loop(0, base_groups // 2, base_pair, 0)
    project(crops, images, 0, width, store_base)
    head_row = lax.shift_right_logical(iota((lanes, heads), 0), pack.bit_length() - 1)
    fold = (head_row == iota((lanes, heads), 1)).astype(bf16)

    def folded(x):
        return sum(dot(piece, fold) for piece in split(x, 3))

    base_peak = folded(by_crop(peak_cols, crops, images))
    base_total = folded(by_crop(total_cols, crops, images))
    all_crops(0, meta_send, meta_recv).wait_recv()

    meta = meta_recv[...].reshape(slots, meta_width)
    unpacked = dot(meta, unpack[...])
    crop_peak = unpacked[:, :heads]
    crop_total = unpacked[:, heads : 2 * heads]
    slot_at = unpacked[:, 2 * heads : 2 * heads + 1]
    across = dot(unpack[...], meta, ((0,), (1,)))
    slot_row = across[2 * heads : 2 * heads + 1, :]
    member = slot_at == iota((slots, images), 1).astype(f32) + 1.0
    member_t = slot_row == iota((images, slots), 0).astype(f32) + 1.0
    joint = base_peak
    for h in range(heads):
        best = jnp.max(jnp.where(member_t, across[h : h + 1, :], very_low), axis=1, keepdims=True)
        joint = jnp.where(iota((images, heads), 1) == h, jnp.maximum(joint, best), joint)
    member_b = jnp.where(member, 1.0, 0.0).astype(bf16)
    member_tb = jnp.where(member_t, 1.0, 0.0).astype(bf16)
    joint_at = sum(dot(member_b, piece) for piece in split(joint, 3))
    taken = slot_at > 0.5
    rescale = jnp.exp(jnp.where(taken, crop_peak - joint_at, very_low))
    base_rescale = jnp.exp(base_peak - joint)
    collected = sum(dot(member_tb, piece) for piece in split(crop_total * rescale, 3))
    inverse = 1.0 / (base_total * base_rescale + collected)
    inverse_at = sum(dot(member_b, piece) for piece in split(inverse, 2))
    crop_factor[...] = sum(dot(piece, widen[...]) for piece in split(rescale * inverse_at, 2))
    base_factor[...] = sum(dot(piece, widen[...]) for piece in split(base_rescale * inverse, 2))
    load_out.wait()
    gathered = [pooled_0, pooled_1, pooled_2]
    features = jnp.zeros((images, width), f32)
    for n, (c0, c1) in enumerate(chunks):
        all_crops(n + 1, *buffers[n]).wait_recv()
        arrived = buffers[n][1][...].reshape(slots, c1 - c0).astype(f32)
        scaled = (arrived * crop_factor[:, c0:c1]).astype(bf16)
        pooled = base_sum[:, c0:c1] * base_factor[:, c0:c1] + dot(member_tb, scaled)
        gathered[n][my_loop] = pooled.astype(bf16)
        share_loop(n + 1, gathered[n])
        features += dot(pooled.astype(bf16), outw[c0:c1, :])
    embed_ref[...] = features.astype(bf16)
    image_unit = unit_rows(features)
    all_loop(0, text_all).wait_recv()

    scale = scale_ref[0]
    bias = bias_ref[0]
    group = loops * images
    texts = text_all[...].reshape(group, wide)
    group_labels = texts[:, width : width + 1].astype(f32)
    sign = jnp.where(group_labels == labels, 1.0, -1.0)
    texts = texts[:, :width]

    def gradient(others, own):
        logits = scale * dot(others, own, ((1,), (1,))) + bias
        tile = (scale * (-sign / (1.0 + jnp.exp(sign * logits)))).astype(bf16)
        return dot(tile, others, ((0,), (0,)))

    image_grad_ref[...] = gradient(texts, image_unit)

    features = jnp.zeros((group, width), f32)
    for n, (c0, c1) in enumerate(chunks):
        all_loop(n + 1, gathered[n]).wait_recv()
        features += dot(gathered[n][...].reshape(group, c1 - c0), outw[c0:c1, :])
    text_grad_ref[...] = gradient(unit_rows(features), text_all[my_loop, :, :width])
    for n, buffer in enumerate([text_all] + gathered):
        all_loop(n, buffer).wait_send()
    for n, (sent, held) in enumerate([(meta_send, meta_recv)] + buffers):
        all_crops(n, sent, held).wait_send()


def hand_over(embed, image_grad, text_grad, embed_out, image_out, text_out, sem):
    copies = [
        pltpu.make_async_copy(source, held, sem.at[i])
        for i, (source, held) in enumerate(
            [(image_grad, image_out), (text_grad, text_out), (embed, embed_out)]
        )
    ]
    for copy in copies:
        copy.start()
    for copy in copies:
        copy.wait()


def per_device(
    crop_tokens,
    crop_lengths,
    crop_owner,
    crop_slot,
    base_tokens,
    key_probe,
    value_weight,
    out_weight,
    text_embed,
    pair_labels,
    logit_scale,
    logit_bias,
):
    owners = lax.axis_size("dp")
    loops = lax.axis_size("loop")
    crops, crop_tok, width = crop_tokens.shape
    images, base_tok, _ = base_tokens.shape
    heads = key_probe.shape[1]
    lanes = heads * pack
    cap = max(2, (2 * crops + owners - 1) // owners)
    cap = -(-cap // 16) * 16
    wide = width + 128
    groups = crops // pack
    chunks = column_chunks(width, heads)
    chunk_buffers = [
        pltpu.VMEM((owners, cap, c1 - c0), bf16) for c0, c1 in chunks
    ]
    vmem = pl.BlockSpec(memory_space=pltpu.VMEM)
    smem = pl.BlockSpec(memory_space=pltpu.SMEM)
    hbm = pl.BlockSpec(memory_space=pl.ANY)
    flops = 2 * (crops * crop_tok + images * base_tok) * width * heads * 2
    flops += 2 * (crops + 2 * images) * width * width
    step = pl.pallas_call(
        functools.partial(step_kernel, (owners, loops, cap)),
        out_shape=(
            pltpu.VMEM((images, width), bf16),
            pltpu.VMEM((images, width), f32),
            pltpu.VMEM((images, width), f32),
        ),
        in_specs=[hbm] * 6 + [smem] * 2 + [hbm] * 4,
        out_specs=(vmem, vmem, vmem),
        scratch_shapes=[
            pltpu.VMEM((1, crops), jnp.int32),
            pltpu.VMEM((1, crops), jnp.int32),
            pltpu.VMEM((1, crops), jnp.int32),
            pltpu.VMEM((heads, width), bf16),
            pltpu.VMEM((images, width), bf16),
            pltpu.VMEM((1, images), jnp.int32),
            pltpu.VMEM(crop_tokens.shape, bf16),
            pltpu.VMEM(base_tokens.shape, bf16),
            pltpu.VMEM((width, width), bf16),
            pltpu.VMEM((width, width), bf16),
            pltpu.VMEM((pack, pack * crop_tok), jnp.int32),
            pltpu.VMEM((crops, 128), f32),
            pltpu.VMEM((heads, crops + images, width), bf16),
            pltpu.VMEM((lanes, lanes), f32),
            pltpu.VMEM((lanes, lanes), f32),
            pltpu.VMEM((crops, width), bf16),
            pltpu.VMEM((images, width), f32),
            pltpu.VMEM((owners * cap, width), f32),
            pltpu.VMEM((images, width), f32),
            pltpu.VMEM((owners, cap, wide - width), bf16),
            pltpu.VMEM((owners, cap, wide - width), bf16),
            *chunk_buffers,
            *chunk_buffers,
            pltpu.VMEM((loops, images, wide), bf16),
            *[pltpu.VMEM((loops, images, c1 - c0), bf16) for c0, c1 in chunks],
            pltpu.VMEM((groups, (heads - heads // 2) * pack, pack * crop_tok), bf16),
            pltpu.VMEM((6 * lanes, wide - width), bf16),
            pltpu.VMEM((crops, wide - width), f32),
            pltpu.VMEM((owners * cap, crops), bf16),
            pltpu.VMEM((wide - width, wide - width), bf16),
            pltpu.VMEM((heads, width), bf16),
            pltpu.SemaphoreType.DMA((groups + 3,)),
            pltpu.SemaphoreType.DMA((6,)),
            pltpu.SemaphoreType.DMA((len(chunks) + 1,)),
            pltpu.SemaphoreType.DMA((len(chunks) + 1,)),
            pltpu.SemaphoreType.DMA((len(chunks) + 1,)),
            pltpu.SemaphoreType.DMA((len(chunks) + 1,)),
        ],
        compiler_params=pltpu.CompilerParams(
            collective_id=0, has_side_effects=True, vmem_limit_bytes=56 * 1024 * 1024
        ),
        cost_estimate=pl.CostEstimate(
            flops=flops, bytes_accessed=17 * 1024 * 1024, transcendentals=0
        ),
        name="contrastive_step",
    )
    results = step(
        crop_lengths,
        crop_owner.reshape(1, crops),
        crop_slot.reshape(1, crops),
        key_probe.T,
        text_embed,
        pair_labels.reshape(1, images),
        logit_scale,
        logit_bias,
        crop_tokens,
        base_tokens,
        value_weight,
        out_weight,
    )
    return pl.pallas_call(
        hand_over,
        out_shape=tuple(jax.ShapeDtypeStruct(r.shape, r.dtype) for r in results),
        in_specs=[vmem] * 3,
        out_specs=(hbm, hbm, hbm),
        scratch_shapes=[pltpu.SemaphoreType.DMA((3,))],
        compiler_params=pltpu.CompilerParams(vmem_limit_bytes=4 * 1024 * 1024),
        name="hand_over",
    )(*results)


def solution(mesh):
    return jax.shard_map(
        per_device,
        mesh=mesh,
        in_specs=(
            P(("dp", "loop"), None, None),
            P(("dp", "loop"), None),
            P(("dp", "loop"), None),
            P(("dp", "loop")),
            P(("dp", "loop"), None, None),
            P(),
            P(),
            P(),
            P(("dp", "loop"), None),
            P(("dp", "loop")),
            P(),
            P(),
        ),
        out_specs=(P(("dp", "loop"), None), P(("dp", "loop"), None), P(("dp", "loop"), None)),
        check_vma=False,
    )
```
